32 devices in a mesh: ctx: 8 (over z, x), grp: 4 (over y, core).
Axes of the slice: x: 2, y: 2, z: 4, core: 2. Of those that a mesh axis runs over, the one named last changes fastest.
Arguments:
- query: bfloat16 [128, 2560], P('ctx', 'grp'), may hold values from -8 to 8
- keys: bfloat16 [32768, 512], P('ctx', 'grp'), may hold values from -16 to 16
- values: bfloat16 [32768, 512], P('ctx', 'grp'), may hold values from -6 to 6
- blocks: int32 [128, 8, 8], P(None, 'ctx'), may hold values from 0 to 31, as said below
Outputs:
- attended: bfloat16 [128, 2560], P(('ctx', 'grp'))
The draws below stay inside these ranges and needn't reach their ends.
Inputs may be any that keep to these rules, and one draw needn't show every extreme that they name: Each row's list for each context shard names 8 different blocks, the first of them block 0.
All inputs are finite; a program needn't handle non-finite values.
Results may differ from the reference program's by a relative error of at most 0.012.
Values may be sent and summed in bfloat16 or wider, within the bound.
A program may use at most 192 MiB of HBM per device.

```python
import math
import jax
import jax.numpy as jnp
from jax import lax

HD = 128
QPK = 5
KVH = 4
QH = 20
ROWS = 128
CTX_DEV = 4096
CTXLEN = 32768
BLOCK = 128
BLK_DEV = 32
SEL = 8


def draw_query(key, part):
    noise_key = jax.random.fold_in(key, 1)
    base = jnp.clip(jax.random.normal(noise_key, (ROWS, QH * HD), jnp.float32), -6.0, 6.0)
    return base.astype(jnp.bfloat16)


def draw_keys(key, part):
    noise_key = jax.random.fold_in(key, 2)
    base = jnp.clip(2.5 * jax.random.normal(noise_key, (CTXLEN, KVH * HD), jnp.float32), -15.0, 15.0)
    return base.astype(jnp.bfloat16)


def draw_blocks(key, part):
    shard_count = CTXLEN // CTX_DEV
    random_bits = jax.random.randint(jax.random.fold_in(key, 3), (ROWS, shard_count, BLK_DEV - 1), 0, 1 << 20)
    distinct = random_bits * BLK_DEV + jnp.arange(BLK_DEV - 1, dtype=jnp.int32)[None, None, :]
    unused, chosen = lax.top_k(distinct, SEL - 1)
    first_block = jnp.zeros((ROWS, shard_count, 1), jnp.int32)
    return jnp.concatenate([first_block, chosen.astype(jnp.int32) + 1], axis=2)


def block_scale(rng, dims, split, smallest, high):
    def one(position, parts):
        draws = jax.random.uniform(jax.random.fold_in(jax.random.fold_in(rng, 6), position), (parts,), jnp.float32, smallest / len(split), high / len(split))
        return jnp.repeat(jnp.exp(draws), dims[position] // parts).reshape((-1,) + (1,) * (len(dims) - position - 1))

    gain = one(*split[0])
    for cut in split[1:]:
        gain = gain * one(*cut)
    return gain


def normal_values(own_key, dims, scale, most, shards=(), kind=jnp.bfloat16):
    values = scale * jax.random.normal(own_key, dims, jnp.float32)
    if shards:
        values = values * block_scale(own_key, dims, shards, -0.22, 0.18)
    return jnp.clip(values, -most, most).astype(kind)


def setup_inputs(seed: int = 0) -> dict:
    splits = jax.random.split(jax.random.key(seed), 5)
    return {
        "query": draw_query(jax.random.fold_in(splits[4], 71), 0),
        "keys": draw_keys(jax.random.fold_in(splits[4], 71), 0),
        "values": normal_values(splits[2], (CTXLEN, KVH * HD), 1.0, 6.0, ((0, 8), (1, 4))),
        "blocks": draw_blocks(jax.random.fold_in(splits[4], 71), 0),
    }


def reference(query, keys, values, blocks):
    shard_count = CTXLEN // CTX_DEV
    score_scale = 1.0 / math.sqrt(HD)
    query_all = query.astype(jnp.float32).reshape(ROWS, KVH, QPK, HD)

    def one_shard(shard):
        start = (shard * CTX_DEV).astype(jnp.int32)
        key_part = lax.dynamic_slice_in_dim(keys, start, CTX_DEV, 0).astype(jnp.float32).reshape(CTX_DEV, KVH, HD)
        value_part = lax.dynamic_slice_in_dim(values, start, CTX_DEV, 0).astype(jnp.float32).reshape(CTX_DEV, KVH, HD)
        listed_here = lax.dynamic_slice_in_dim(blocks, shard.astype(jnp.int32), 1, 1)[:, 0, :]
        block_ids = jnp.arange(BLK_DEV, dtype=jnp.int32)
        block_hits = jnp.any(listed_here[:, :, None] == block_ids[None, None, :], axis=1)
        token_mask = jnp.repeat(block_hits, BLOCK, axis=1)[:, None, None, :]
        scores = jnp.einsum('rgqd,tgd->rgqt', query_all, key_part) * score_scale
        local_max = lax.optimization_barrier(jnp.max(jnp.where(token_mask, scores, -jnp.inf), axis=-1))
        weights = jnp.where(token_mask, jnp.exp(scores - local_max[..., None]), 0.0)
        local_sum = lax.optimization_barrier(jnp.sum(weights, axis=-1))
        rounded = lax.optimization_barrier(weights.astype(jnp.bfloat16)).astype(jnp.float32)
        local_out = jnp.einsum('rgqt,tgd->rgqd', rounded, value_part)
        part_out = lax.optimization_barrier((local_out / local_sum[..., None]).astype(jnp.bfloat16)).astype(jnp.float32)
        log_total = local_max + jnp.log(local_sum)
        return (log_total, part_out)
    all_lse, all_part = lax.map(one_shard, jnp.arange(shard_count, dtype=jnp.int32))
    top_lse = lax.optimization_barrier(jnp.max(all_lse, axis=0))
    factor = jnp.exp(all_lse - top_lse[None])
    denominator = lax.optimization_barrier(jnp.sum(factor, axis=0))
    numerator = lax.optimization_barrier(jnp.sum(factor[..., None] * all_part, axis=0))
    result = numerator / denominator[..., None]
    return result.reshape(ROWS, QH * HD).astype(jnp.bfloat16)
```

```python
import functools
import math

import jax
import jax.numpy as jnp
from jax import lax
from jax.experimental import pallas as pl
from jax.experimental.pallas import tpu as pltpu
from jax.sharding import PartitionSpec as P

HD = 128
QPK = 5
BLOCK = 128
LANES = 128
NEG = -1e30
PAD = 16
SLOTS_PER_TURN = 2
CHUNK = 1024
MESH = pl.DeviceIdType.MESH


def xor(a, b, n):
    total, bit = 0, 1
    while bit < n:
        total = total + bit * ((a // bit + b // bit) % 2)
        bit *= 2
    return total


def kernel(
    n, ng, q_ref, k_ref, v_ref, b_ref, o_ref,
    qbuf, kext, vext, mask, score, part_out, part_in, fin_out, fin_in,
    local_sem, qsend, qrecv, psend, precv, fsend, frecv,
):
    me = lax.axis_index("ctx")
    grp = lax.axis_index("grp")
    own_rows = qbuf.shape[1]
    group_rows = QPK * own_rows
    tokens = kext.shape[0]
    row_count = mask.shape[0]
    log2_scale = math.log2(math.e) / math.sqrt(HD)

    barrier = pltpu.get_barrier_semaphore()
    for k in range(1, n):
        pl.semaphore_signal(barrier, inc=1, device_id={"ctx": xor(me, k, n)}, device_id_type=MESH)
    for j in range(1, ng):
        pl.semaphore_signal(barrier, inc=1, device_id={"grp": xor(grp, j, ng)}, device_id_type=MESH)

    load_q = pltpu.make_async_copy(q_ref, qbuf.at[0], local_sem.at[0])
    load_k = pltpu.make_async_copy(k_ref, kext.at[:, 0:HD], local_sem.at[1])
    load_v = pltpu.make_async_copy(v_ref, vext.at[:, 0:HD], local_sem.at[2])
    load_q.start()
    load_k.start()
    load_v.start()

    def query_copy(k):
        return pltpu.make_async_remote_copy(
            src_ref=qbuf.at[0], dst_ref=qbuf.at[k], send_sem=qsend.at[k], recv_sem=qrecv.at[k],
            device_id={"ctx": xor(me, k, n)}, device_id_type=MESH,
        )

    def part_copy(k):
        return pltpu.make_async_remote_copy(
            src_ref=part_out.at[k], dst_ref=part_in.at[k], send_sem=psend.at[k], recv_sem=precv.at[k],
            device_id={"ctx": xor(me, k, n)}, device_id_type=MESH,
        )

    def fin_copy(j):
        return pltpu.make_async_remote_copy(
            src_ref=fin_out, dst_ref=fin_in.at[j], send_sem=fsend.at[j], recv_sem=frecv.at[j],
            device_id={"grp": xor(grp, j, ng)}, device_id_type=MESH,
        )

    pl.semaphore_wait(barrier, n - 1 + ng - 1)
    load_q.wait()
    for k in range(1, n):
        query_copy(k).start()

    lane = lax.broadcasted_iota(jnp.int32, (BLOCK, LANES), 1)
    for b in range(tokens // BLOCK):
        kext[b * BLOCK:(b + 1) * BLOCK, HD:] = jnp.where(lane == b, 1.0, 0.0).astype(jnp.bfloat16)
    vext[:, HD:] = jnp.ones((tokens, LANES), jnp.bfloat16)
    listed = b_ref[...]
    block_row = lax.broadcasted_iota(jnp.int32, (tokens // BLOCK, row_count), 0)
    hit = block_row == listed[0:1, :]
    for i in range(1, listed.shape[0]):
        hit = hit | (block_row == listed[i:i + 1, :])
    bias = jnp.where(hit, 0.0, NEG)
    unused = jnp.zeros((LANES - tokens // BLOCK, row_count), jnp.float32)
    mask[...] = jnp.transpose(jnp.concatenate([bias, unused], axis=0)).astype(jnp.bfloat16)

    diag = (
        lax.broadcasted_iota(jnp.int32, (group_rows, LANES), 0)
        == lax.broadcasted_iota(jnp.int32, (group_rows, LANES), 1)
    )
    pad_row = lax.broadcasted_iota(jnp.int32, (PAD, LANES), 0)
    load_k.wait()
    load_v.wait()

    def turn(t, carry):
        pieces = []
        for u in range(SLOTS_PER_TURN):
            k = t * SLOTS_PER_TURN + u

            @pl.when(k > 0)
            def _():
                query_copy(k).wait_recv()

            owner = xor(me, k, n)
            bias = mask[pl.ds(pl.multiple_of(owner * own_rows, own_rows), own_rows), :]
            rows = qbuf[k]
            for h in range(QPK):
                pieces.append(jnp.concatenate([rows[:, h * HD:(h + 1) * HD], bias], axis=1))
        query = jnp.concatenate(pieces, axis=0)
        top = None
        for c in range(0, tokens, CHUNK):
            s = lax.dot_general(
                query, kext[c:c + CHUNK, :], (((1,), (1,)), ((), ())), preferred_element_type=jnp.float32
            )
            score[:, c:c + CHUNK] = s
            for i in range(0, CHUNK, LANES):
                part = s[:, i:i + LANES]
                top = part if top is None else jnp.maximum(top, part)
        top = jnp.max(top, axis=1, keepdims=True)
        total = None
        for c in range(0, tokens, CHUNK):
            w = jnp.exp2((score[:, c:c + CHUNK] - top) * log2_scale).astype(jnp.bfloat16)
            piece = jnp.dot(w, vext[c:c + CHUNK, :], preferred_element_type=jnp.float32)
            total = piece if total is None else total + piece
        weight = total[:, HD:]
        part = (total[:, :HD] / weight).astype(jnp.bfloat16)
        lse = top * (1.0 / math.sqrt(HD)) + jnp.log(weight)
        for u in range(SLOTS_PER_TURN):
            k = t * SLOTS_PER_TURN + u
            at = slice(u * group_rows, (u + 1) * group_rows)
            line = jnp.sum(jnp.where(diag, lse[at], 0.0), axis=0, keepdims=True)
            high = line.astype(jnp.bfloat16).astype(jnp.float32)
            mid = (line - high).astype(jnp.bfloat16).astype(jnp.float32)
            low = line - high - mid
            tail = jnp.where(pad_row == 0, high, jnp.where(pad_row == 1, mid, jnp.where(pad_row == 2, low, 0.0)))
            part_out[k, 0:group_rows, :] = part[at]
            part_out[k, group_rows:, :] = tail.astype(jnp.bfloat16)

            @pl.when(k > 0)
            def _():
                part_copy(k).start()

        return carry

    lax.fori_loop(0, n // SLOTS_PER_TURN, turn, 0)

    for k in range(1, n):
        part_copy(k).wait_recv()
    parts = [part_out.at[0]] + [part_in.at[k] for k in range(1, n)]
    lines = [jnp.sum(p[group_rows:, :].astype(jnp.float32), axis=0, keepdims=True) for p in parts]
    best = functools.reduce(jnp.maximum, lines)
    factors = [jnp.exp(x - best) for x in lines]
    denominator = sum(factors[1:], factors[0])
    factors.append(jnp.zeros((LANES - n, LANES), jnp.float32))
    columns = jnp.transpose(jnp.concatenate(factors, axis=0) / denominator)
    result = None
    for k, p in enumerate(parts):
        piece = p[0:group_rows, :].astype(jnp.float32) * columns[0:group_rows, k:k + 1]
        result = piece if result is None else result + piece
    for h in range(QPK):
        fin_out[:, h * HD:(h + 1) * HD] = result[h * own_rows:(h + 1) * own_rows].astype(jnp.bfloat16)
    for j in range(1, ng):
        fin_copy(j).start()

    out_rows = own_rows // ng
    width = QPK * HD
    for j in range(ng):
        if j > 0:
            fin_copy(j).wait_recv()
        whole = (fin_out if j == 0 else fin_in.at[j])[...].astype(jnp.float32)
        mine = whole[0:out_rows]
        for g in range(1, ng):
            mine = jnp.where(grp == g, whole[g * out_rows:(g + 1) * out_rows], mine)
        origin = xor(grp, j, ng)
        o_ref[:, pl.ds(pl.multiple_of(origin * width, LANES), width)] = mine.astype(jnp.bfloat16)

    for k in range(1, n):
        query_copy(k).wait_send()
        part_copy(k).wait_send()
    for j in range(1, ng):
        fin_copy(j).wait_send()


def per_device(n, ng, query, keys, values, blocks):
    own_rows, width = query.shape
    tokens = keys.shape[0]
    rows = blocks.shape[0]
    message = QPK * own_rows + PAD
    any_spec = pl.BlockSpec(memory_space=pl.ANY)
    vmem_spec = pl.BlockSpec(memory_space=pltpu.VMEM)
    return pl.pallas_call(
        functools.partial(kernel, n, ng),
        out_shape=jax.ShapeDtypeStruct((own_rows // ng, width * ng), jnp.bfloat16),
        in_specs=[any_spec, any_spec, any_spec, vmem_spec],
        out_specs=vmem_spec,
        scratch_shapes=[
            pltpu.VMEM((n, own_rows, width), jnp.bfloat16),
            pltpu.VMEM((tokens, 2 * HD), jnp.bfloat16),
            pltpu.VMEM((tokens, 2 * HD), jnp.bfloat16),
            pltpu.VMEM((rows, LANES), jnp.bfloat16),
            pltpu.VMEM((SLOTS_PER_TURN * QPK * own_rows, tokens), jnp.float32),
            pltpu.VMEM((n, message, HD), jnp.bfloat16),
            pltpu.VMEM((n, message, HD), jnp.bfloat16),
            pltpu.VMEM((own_rows, width), jnp.bfloat16),
            pltpu.VMEM((ng, own_rows, width), jnp.bfloat16),
            pltpu.SemaphoreType.DMA((3,)),
            pltpu.SemaphoreType.DMA((n,)),
            pltpu.SemaphoreType.DMA((n,)),
            pltpu.SemaphoreType.DMA((n,)),
            pltpu.SemaphoreType.DMA((n,)),
            pltpu.SemaphoreType.DMA((ng,)),
            pltpu.SemaphoreType.DMA((ng,)),
        ],
        compiler_params=pltpu.CompilerParams(
            collective_id=0, has_side_effects=True, vmem_limit_bytes=60 * 1024 * 1024
        ),
    )(query, keys, values, jnp.transpose(blocks, (1, 2, 0))[0])


def solution(mesh):
    placed = (P("ctx", "grp"), P("ctx", "grp"), P("ctx", "grp"), P(None, "ctx", None))
    body = functools.partial(per_device, mesh.shape["ctx"], mesh.shape["grp"])
    return jax.shard_map(
        body, mesh=mesh, in_specs=placed, out_specs=P(("ctx", "grp"), None), check_vma=False
    )
```

```python
import functools
import math

import jax
import jax.numpy as jnp
from jax import lax
from jax.experimental import pallas as pl
from jax.experimental.pallas import tpu as pltpu
from jax.sharding import PartitionSpec as P

HD = 128
QPK = 5
BLOCK = 128
LANES = 128
NEG = -1e30
PAD = 16
SLOTS_PER_TURN = 2
CHUNK = 1024
MESH = pl.DeviceIdType.MESH


def xor(a, b, n):
    total, bit = 0, 1
    while bit < n:
        total = total + bit * ((a // bit + b // bit) % 2)
        bit *= 2
    return total


def kernel(
    n, ng, q_ref, k_ref, v_ref, b_ref, o_ref,
    qbuf, kbuf, kext, vext, mask, score, part_out, part_in, fin_out, fin_in,
    local_sem, qsend, qrecv, psend, precv, fsend, frecv,
):
    me = lax.axis_index("ctx")
    grp = lax.axis_index("grp")
    own_rows = qbuf.shape[1]
    group_rows = QPK * own_rows
    tokens = kbuf.shape[0]
    row_count = mask.shape[0]
    scale = 1.0 / math.sqrt(HD)

    barrier = pltpu.get_barrier_semaphore()
    for k in range(1, n):
        pl.semaphore_signal(barrier, inc=1, device_id={"ctx": xor(me, k, n)}, device_id_type=MESH)
    for j in range(1, ng):
        pl.semaphore_signal(barrier, inc=1, device_id={"grp": xor(grp, j, ng)}, device_id_type=MESH)

    load_q = pltpu.make_async_copy(q_ref, qbuf.at[0], local_sem.at[0])
    load_k = pltpu.make_async_copy(k_ref, kbuf, local_sem.at[1])
    load_v = pltpu.make_async_copy(v_ref, vext.at[:, 0:HD], local_sem.at[2])
    load_q.start()
    load_k.start()
    load_v.start()

    def query_copy(k):
        return pltpu.make_async_remote_copy(
            src_ref=qbuf.at[0], dst_ref=qbuf.at[k], send_sem=qsend.at[k], recv_sem=qrecv.at[k],
            device_id={"ctx": xor(me, k, n)}, device_id_type=MESH,
        )

    def part_copy(k):
        return pltpu.make_async_remote_copy(
            src_ref=part_out.at[k], dst_ref=part_in.at[k], send_sem=psend.at[k], recv_sem=precv.at[k],
            device_id={"ctx": xor(me, k, n)}, device_id_type=MESH,
        )

    def fin_copy(j):
        return pltpu.make_async_remote_copy(
            src_ref=fin_out, dst_ref=fin_in.at[j], send_sem=fsend.at[j], recv_sem=frecv.at[j],
            device_id={"grp": xor(grp, j, ng)}, device_id_type=MESH,
        )

    pl.semaphore_wait(barrier, n - 1 + ng - 1)
    load_q.wait()
    for k in range(1, n):
        query_copy(k).start()

    sub = lax.broadcasted_iota(jnp.int32, (LANES, BLOCK), 0)
    for b in range(tokens // BLOCK):
        kext[HD:, b * BLOCK:(b + 1) * BLOCK] = jnp.where(sub == b, 1.0, 0.0).astype(jnp.bfloat16)
    vext[:, HD:] = jnp.ones((tokens, LANES), jnp.bfloat16)
    listed = b_ref[...]
    block_row = lax.broadcasted_iota(jnp.int32, (tokens // BLOCK, row_count), 0)
    hit = block_row == listed[0:1, :]
    for i in range(1, listed.shape[0]):
        hit = hit | (block_row == listed[i:i + 1, :])
    bias = jnp.where(hit, 0.0, NEG)
    unused = jnp.zeros((LANES - tokens // BLOCK, row_count), jnp.float32)
    mask[...] = jnp.transpose(jnp.concatenate([bias, unused], axis=0)).astype(jnp.bfloat16)

    diag = (
        lax.broadcasted_iota(jnp.int32, (group_rows, LANES), 0)
        == lax.broadcasted_iota(jnp.int32, (group_rows, LANES), 1)
    )
    pad_row = lax.broadcasted_iota(jnp.int32, (PAD, LANES), 0)
    load_k.wait()
    for b in range(tokens // BLOCK):
        at = slice(b * BLOCK, (b + 1) * BLOCK)
        kext[0:HD, at] = jnp.transpose(kbuf[at, :].astype(jnp.float32)).astype(jnp.bfloat16)
    load_v.wait()

    def turn(t, carry):
        pieces = []
        for u in range(SLOTS_PER_TURN):
            k = t * SLOTS_PER_TURN + u

            @pl.when(k > 0)
            def _():
                query_copy(k).wait_recv()

            owner = xor(me, k, n)
            bias = mask[pl.ds(pl.multiple_of(owner * own_rows, own_rows), own_rows), :]
            rows = qbuf[k]
            for h in range(QPK):
                pieces.append(jnp.concatenate([rows[:, h * HD:(h + 1) * HD], bias], axis=1))
        query = jnp.concatenate(pieces, axis=0)
        top = None
        for c in range(0, tokens, CHUNK):
            s = jnp.dot(query, kext[:, c:c + CHUNK], preferred_element_type=jnp.float32)
            score[:, c:c + CHUNK] = s
            for i in range(0, CHUNK, LANES):
                part = s[:, i:i + LANES]
                top = part if top is None else jnp.maximum(top, part)
        top = jnp.max(top, axis=1, keepdims=True)
        total = None
        for c in range(0, tokens, CHUNK):
            w = jnp.exp((score[:, c:c + CHUNK] - top) * scale).astype(jnp.bfloat16)
            piece = jnp.dot(w, vext[c:c + CHUNK, :], preferred_element_type=jnp.float32)
            total = piece if total is None else total + piece
        weight = total[:, HD:]
        part = (total[:, :HD] / weight).astype(jnp.bfloat16)
        lse = top * scale + jnp.log(weight)
        for u in range(SLOTS_PER_TURN):
            k = t * SLOTS_PER_TURN + u
            at = slice(u * group_rows, (u + 1) * group_rows)
            line = jnp.sum(jnp.where(diag, lse[at], 0.0), axis=0, keepdims=True)
            high = line.astype(jnp.bfloat16).astype(jnp.float32)
            mid = (line - high).astype(jnp.bfloat16).astype(jnp.float32)
            low = line - high - mid
            tail = jnp.where(pad_row == 0, high, jnp.where(pad_row == 1, mid, jnp.where(pad_row == 2, low, 0.0)))
            part_out[k, 0:group_rows, :] = part[at]
            part_out[k, group_rows:, :] = tail.astype(jnp.bfloat16)

            @pl.when(k > 0)
            def _():
                part_copy(k).start()

        return carry

    lax.fori_loop(0, n // SLOTS_PER_TURN, turn, 0)

    for k in range(1, n):
        part_copy(k).wait_recv()
    parts = [part_out.at[0]] + [part_in.at[k] for k in range(1, n)]
    lines = [jnp.sum(p[group_rows:, :].astype(jnp.float32), axis=0, keepdims=True) for p in parts]
    best = functools.reduce(jnp.maximum, lines)
    factors = [jnp.exp(x - best) for x in lines]
    denominator = sum(factors[1:], factors[0])
    factors.append(jnp.zeros((LANES - n, LANES), jnp.float32))
    columns = jnp.transpose(jnp.concatenate(factors, axis=0) / denominator)
    result = None
    for k, p in enumerate(parts):
        piece = p[0:group_rows, :].astype(jnp.float32) * columns[0:group_rows, k:k + 1]
        result = piece if result is None else result + piece
    for h in range(QPK):
        fin_out[:, h * HD:(h + 1) * HD] = result[h * own_rows:(h + 1) * own_rows].astype(jnp.bfloat16)
    for j in range(1, ng):
        fin_copy(j).start()

    out_rows = own_rows // ng
    width = QPK * HD
    for j in range(ng):
        if j > 0:
            fin_copy(j).wait_recv()
        whole = (fin_out if j == 0 else fin_in.at[j])[...].astype(jnp.float32)
        mine = whole[0:out_rows]
        for g in range(1, ng):
            mine = jnp.where(grp == g, whole[g * out_rows:(g + 1) * out_rows], mine)
        origin = xor(grp, j, ng)
        o_ref[:, pl.ds(pl.multiple_of(origin * width, LANES), width)] = mine.astype(jnp.bfloat16)

    for k in range(1, n):
        query_copy(k).wait_send()
        part_copy(k).wait_send()
    for j in range(1, ng):
        fin_copy(j).wait_send()


def per_device(n, ng, query, keys, values, blocks):
    own_rows, width = query.shape
    tokens = keys.shape[0]
    rows = blocks.shape[0]
    message = QPK * own_rows + PAD
    any_spec = pl.BlockSpec(memory_space=pl.ANY)
    vmem_spec = pl.BlockSpec(memory_space=pltpu.VMEM)
    return pl.pallas_call(
        functools.partial(kernel, n, ng),
        out_shape=jax.ShapeDtypeStruct((own_rows // ng, width * ng), jnp.bfloat16),
        in_specs=[any_spec, any_spec, any_spec, vmem_spec],
        out_specs=vmem_spec,
        scratch_shapes=[
            pltpu.VMEM((n, own_rows, width), jnp.bfloat16),
            pltpu.VMEM((tokens, HD), jnp.bfloat16),
            pltpu.VMEM((2 * HD, tokens), jnp.bfloat16),
            pltpu.VMEM((tokens, 2 * HD), jnp.bfloat16),
            pltpu.VMEM((rows, LANES), jnp.bfloat16),
            pltpu.VMEM((SLOTS_PER_TURN * QPK * own_rows, tokens), jnp.float32),
            pltpu.VMEM((n, message, HD), jnp.bfloat16),
            pltpu.VMEM((n, message, HD), jnp.bfloat16),
            pltpu.VMEM((own_rows, width), jnp.bfloat16),
            pltpu.VMEM((ng, own_rows, width), jnp.bfloat16),
            pltpu.SemaphoreType.DMA((3,)),
            pltpu.SemaphoreType.DMA((n,)),
            pltpu.SemaphoreType.DMA((n,)),
            pltpu.SemaphoreType.DMA((n,)),
            pltpu.SemaphoreType.DMA((n,)),
            pltpu.SemaphoreType.DMA((ng,)),
            pltpu.SemaphoreType.DMA((ng,)),
        ],
        compiler_params=pltpu.CompilerParams(
            collective_id=0, has_side_effects=True, vmem_limit_bytes=60 * 1024 * 1024
        ),
    )(query, keys, values, jnp.transpose(blocks, (1, 2, 0))[0])


def solution(mesh):
    placed = (P("ctx", "grp"), P("ctx", "grp"), P("ctx", "grp"), P(None, "ctx", None))
    body = functools.partial(per_device, mesh.shape["ctx"], mesh.shape["grp"])
    return jax.shard_map(
        body, mesh=mesh, in_specs=placed, out_specs=P(("ctx", "grp"), None), check_vma=False
    )
```

```python
import functools
import math

import jax
import jax.numpy as jnp
from jax import lax
from jax.experimental import pallas as pl
from jax.experimental.pallas import tpu as pltpu
from jax.sharding import PartitionSpec as P

HD = 128
QPK = 5
BLOCK = 128
LANES = 128
NEG = -1e30
PAD = 16
SLOTS_PER_TURN = 2
CHUNK = 256
MESH = pl.DeviceIdType.MESH


def xor(a, b, n):
    total, bit = 0, 1
    while bit < n:
        total = total + bit * ((a // bit + b // bit) % 2)
        bit *= 2
    return total


def kernel(
    n, ng, q_ref, k_ref, v_ref, b_ref, o_ref,
    qbuf, kbuf, kext, vext, mask, score, rounded, part_out, part_in, fin_out, fin_in,
    local_sem, qsend, qrecv, psend, precv, fsend, frecv,
):
    me = lax.axis_index("ctx")
    grp = lax.axis_index("grp")
    own_rows = qbuf.shape[1]
    group_rows = QPK * own_rows
    tokens = kbuf.shape[0]
    row_count = mask.shape[0]
    scale = 1.0 / math.sqrt(HD)

    barrier = pltpu.get_barrier_semaphore()
    for k in range(1, n):
        pl.semaphore_signal(barrier, inc=1, device_id={"ctx": xor(me, k, n)}, device_id_type=MESH)
    for j in range(1, ng):
        pl.semaphore_signal(barrier, inc=1, device_id={"grp": xor(grp, j, ng)}, device_id_type=MESH)

    load_q = pltpu.make_async_copy(q_ref, qbuf.at[0], local_sem.at[0])
    load_k = pltpu.make_async_copy(k_ref, kbuf, local_sem.at[1])
    load_v = pltpu.make_async_copy(v_ref, vext.at[:, 0:HD], local_sem.at[2])
    load_q.start()
    load_k.start()
    load_v.start()

    def query_copy(k):
        return pltpu.make_async_remote_copy(
            src_ref=qbuf.at[0], dst_ref=qbuf.at[k], send_sem=qsend.at[k], recv_sem=qrecv.at[k],
            device_id={"ctx": xor(me, k, n)}, device_id_type=MESH,
        )

    def part_copy(k):
        return pltpu.make_async_remote_copy(
            src_ref=part_out.at[k], dst_ref=part_in.at[k], send_sem=psend.at[k], recv_sem=precv.at[k],
            device_id={"ctx": xor(me, k, n)}, device_id_type=MESH,
        )

    def fin_copy(j):
        return pltpu.make_async_remote_copy(
            src_ref=fin_out, dst_ref=fin_in.at[j], send_sem=fsend.at[j], recv_sem=frecv.at[j],
            device_id={"grp": xor(grp, j, ng)}, device_id_type=MESH,
        )

    pl.semaphore_wait(barrier, n - 1 + ng - 1)
    load_q.wait()
    for k in range(1, n):
        query_copy(k).start()

    sub = lax.broadcasted_iota(jnp.int32, (LANES, BLOCK), 0)
    for b in range(tokens // BLOCK):
        kext[HD:, b * BLOCK:(b + 1) * BLOCK] = jnp.where(sub == b, 1.0, 0.0).astype(jnp.bfloat16)
    vext[:, HD:] = jnp.ones((tokens, LANES), jnp.bfloat16)
    listed = b_ref[...]
    block_row = lax.broadcasted_iota(jnp.int32, (tokens // BLOCK, row_count), 0)
    hit = block_row == listed[0:1, :]
    for i in range(1, listed.shape[0]):
        hit = hit | (block_row == listed[i:i + 1, :])
    bias = jnp.where(hit, 0.0, NEG)
    unused = jnp.zeros((LANES - tokens // BLOCK, row_count), jnp.float32)
    mask[...] = jnp.transpose(jnp.concatenate([bias, unused], axis=0)).astype(jnp.bfloat16)

    diag = (
        lax.broadcasted_iota(jnp.int32, (group_rows, LANES), 0)
        == lax.broadcasted_iota(jnp.int32, (group_rows, LANES), 1)
    )
    pad_row = lax.broadcasted_iota(jnp.int32, (PAD, LANES), 0)
    load_k.wait()
    for b in range(tokens // BLOCK):
        at = slice(b * BLOCK, (b + 1) * BLOCK)
        kext[0:HD, at] = jnp.transpose(kbuf[at, :].astype(jnp.float32)).astype(jnp.bfloat16)
    load_v.wait()

    def turn(t, carry):
        pieces = []
        for u in range(SLOTS_PER_TURN):
            k = t * SLOTS_PER_TURN + u

            @pl.when(k > 0)
            def _():
                query_copy(k).wait_recv()

            owner = xor(me, k, n)
            bias = mask[pl.ds(pl.multiple_of(owner * own_rows, own_rows), own_rows), :]
            rows = qbuf[k]
            for h in range(QPK):
                pieces.append(jnp.concatenate([rows[:, h * HD:(h + 1) * HD], bias], axis=1))
        query = jnp.concatenate(pieces, axis=0)
        top = None
        for c in range(0, tokens, CHUNK):
            s = jnp.dot(query, kext[:, c:c + CHUNK], preferred_element_type=jnp.float32)
            score[:, c:c + CHUNK] = s
            for i in range(0, CHUNK, LANES):
                part = s[:, i:i + LANES]
                top = part if top is None else jnp.maximum(top, part)
        top = jnp.max(top, axis=1, keepdims=True)
        for c in range(0, tokens, CHUNK):
            at = slice(c, c + CHUNK)
            rounded[:, at] = jnp.exp((score[:, at] - top) * scale).astype(jnp.bfloat16)
        total = jnp.dot(rounded[...], vext[...], preferred_element_type=jnp.float32)
        weight = total[:, HD:]
        part = (total[:, :HD] / weight).astype(jnp.bfloat16)
        lse = top * scale + jnp.log(weight)
        for u in range(SLOTS_PER_TURN):
            k = t * SLOTS_PER_TURN + u
            at = slice(u * group_rows, (u + 1) * group_rows)
            line = jnp.sum(jnp.where(diag, lse[at], 0.0), axis=0, keepdims=True)
            high = line.astype(jnp.bfloat16).astype(jnp.float32)
            mid = (line - high).astype(jnp.bfloat16).astype(jnp.float32)
            low = line - high - mid
            tail = jnp.where(pad_row == 0, high, jnp.where(pad_row == 1, mid, jnp.where(pad_row == 2, low, 0.0)))
            part_out[k, 0:group_rows, :] = part[at]
            part_out[k, group_rows:, :] = tail.astype(jnp.bfloat16)

            @pl.when(k > 0)
            def _():
                part_copy(k).start()

        return carry

    lax.fori_loop(0, n // SLOTS_PER_TURN, turn, 0)

    for k in range(1, n):
        part_copy(k).wait_recv()
    parts = [part_out.at[0]] + [part_in.at[k] for k in range(1, n)]
    lines = [jnp.sum(p[group_rows:, :].astype(jnp.float32), axis=0, keepdims=True) for p in parts]
    best = functools.reduce(jnp.maximum, lines)
    factors = [jnp.exp(x - best) for x in lines]
    denominator = sum(factors[1:], factors[0])
    factors.append(jnp.zeros((LANES - n, LANES), jnp.float32))
    columns = jnp.transpose(jnp.concatenate(factors, axis=0) / denominator)
    result = None
    for k, p in enumerate(parts):
        piece = p[0:group_rows, :].astype(jnp.float32) * columns[0:group_rows, k:k + 1]
        result = piece if result is None else result + piece
    for h in range(QPK):
        fin_out[:, h * HD:(h + 1) * HD] = result[h * own_rows:(h + 1) * own_rows].astype(jnp.bfloat16)
    for j in range(1, ng):
        fin_copy(j).start()

    out_rows = own_rows // ng
    width = QPK * HD
    for j in range(ng):
        if j > 0:
            fin_copy(j).wait_recv()
        whole = (fin_out if j == 0 else fin_in.at[j])[...].astype(jnp.float32)
        mine = whole[0:out_rows]
        for g in range(1, ng):
            mine = jnp.where(grp == g, whole[g * out_rows:(g + 1) * out_rows], mine)
        origin = xor(grp, j, ng)
        o_ref[:, pl.ds(pl.multiple_of(origin * width, LANES), width)] = mine.astype(jnp.bfloat16)

    for k in range(1, n):
        query_copy(k).wait_send()
        part_copy(k).wait_send()
    for j in range(1, ng):
        fin_copy(j).wait_send()


def per_device(n, ng, query, keys, values, blocks):
    own_rows, width = query.shape
    tokens = keys.shape[0]
    rows = blocks.shape[0]
    message = QPK * own_rows + PAD
    any_spec = pl.BlockSpec(memory_space=pl.ANY)
    vmem_spec = pl.BlockSpec(memory_space=pltpu.VMEM)
    return pl.pallas_call(
        functools.partial(kernel, n, ng),
        out_shape=jax.ShapeDtypeStruct((own_rows // ng, width * ng), jnp.bfloat16),
        in_specs=[any_spec, any_spec, any_spec, vmem_spec],
        out_specs=vmem_spec,
        scratch_shapes=[
            pltpu.VMEM((n, own_rows, width), jnp.bfloat16),
            pltpu.VMEM((tokens, HD), jnp.bfloat16),
            pltpu.VMEM((2 * HD, tokens), jnp.bfloat16),
            pltpu.VMEM((tokens, 2 * HD), jnp.bfloat16),
            pltpu.VMEM((rows, LANES), jnp.bfloat16),
            pltpu.VMEM((SLOTS_PER_TURN * QPK * own_rows, tokens), jnp.float32),
            pltpu.VMEM((SLOTS_PER_TURN * QPK * own_rows, tokens), jnp.bfloat16),
            pltpu.VMEM((n, message, HD), jnp.bfloat16),
            pltpu.VMEM((n, message, HD), jnp.bfloat16),
            pltpu.VMEM((own_rows, width), jnp.bfloat16),
            pltpu.VMEM((ng, own_rows, width), jnp.bfloat16),
            pltpu.SemaphoreType.DMA((3,)),
            pltpu.SemaphoreType.DMA((n,)),
            pltpu.SemaphoreType.DMA((n,)),
            pltpu.SemaphoreType.DMA((n,)),
            pltpu.SemaphoreType.DMA((n,)),
            pltpu.SemaphoreType.DMA((ng,)),
            pltpu.SemaphoreType.DMA((ng,)),
        ],
        compiler_params=pltpu.CompilerParams(
            collective_id=0, has_side_effects=True, vmem_limit_bytes=60 * 1024 * 1024
        ),
    )(query, keys, values, jnp.transpose(blocks, (1, 2, 0))[0])


def solution(mesh):
    placed = (P("ctx", "grp"), P("ctx", "grp"), P("ctx", "grp"), P(None, "ctx", None))
    body = functools.partial(per_device, mesh.shape["ctx"], mesh.shape["grp"])
    return jax.shard_map(
        body, mesh=mesh, in_specs=placed, out_specs=P(("ctx", "grp"), None), check_vma=False
    )
```

```python
import functools
import math

import jax
import jax.numpy as jnp
from jax import lax
from jax.experimental import pallas as pl
from jax.experimental.pallas import tpu as pltpu
from jax.sharding import PartitionSpec as P

HD = 128
QPK = 5
BLOCK = 128
LANES = 128
NEG = -1e30
PAD = 16
SLOTS_PER_TURN = 2
CHUNK = 1024
MESH = pl.DeviceIdType.MESH


def xor(a, b, n):
    total, bit = 0, 1
    while bit < n:
        total = total + bit * ((a // bit + b // bit) % 2)
        bit *= 2
    return total


def kernel(
    n, ng, q_ref, k_ref, v_ref, b_ref, o_ref,
    qbuf, kbuf, kext, vext, mask, score, part_out, part_in,
    local_sem, qsend, qrecv, psend, precv, ready,
):
    me = lax.axis_index("ctx")
    grp = lax.axis_index("grp")
    own_rows = qbuf.shape[1]
    group_rows = QPK * own_rows
    tokens = kbuf.shape[0]
    message = part_in.shape[2]
    out_rows = own_rows // ng
    piece_rows = QPK * out_rows
    row_count = mask.shape[0]
    scale = 1.0 / math.sqrt(HD)

    barrier = pltpu.get_barrier_semaphore()
    for k in range(1, n):
        pl.semaphore_signal(barrier, inc=1, device_id={"ctx": xor(me, k, n)}, device_id_type=MESH)
    for j in range(1, ng):
        pl.semaphore_signal(barrier, inc=1, device_id={"grp": xor(grp, j, ng)}, device_id_type=MESH)

    load_q = pltpu.make_async_copy(q_ref, qbuf.at[0], local_sem.at[0])
    load_k = pltpu.make_async_copy(k_ref, kbuf, local_sem.at[1])
    load_v = pltpu.make_async_copy(v_ref, vext.at[:, 0:HD], local_sem.at[2])
    load_q.start()
    load_k.start()
    load_v.start()

    def query_copy(k):
        return pltpu.make_async_remote_copy(
            src_ref=qbuf.at[0], dst_ref=qbuf.at[k], send_sem=qsend.at[k], recv_sem=qrecv.at[k],
            device_id={"ctx": xor(me, k, n)}, device_id_type=MESH,
        )

    def part_copy(k, j):
        target = xor(grp, j, ng)
        return pltpu.make_async_remote_copy(
            src_ref=part_out.at[k, pl.ds(pl.multiple_of(target * message, PAD), message)],
            dst_ref=part_in.at[k, j], send_sem=psend.at[k, j], recv_sem=precv.at[k, j],
            device_id={"ctx": xor(me, k, n), "grp": target}, device_id_type=MESH,
        )

    pl.semaphore_wait(barrier, n - 1 + ng - 1)
    for j in range(1, ng):
        pl.semaphore_signal(ready, inc=1, device_id={"grp": xor(grp, j, ng)}, device_id_type=MESH)
    load_q.wait()
    for k in range(1, n):
        query_copy(k).start()

    sub = lax.broadcasted_iota(jnp.int32, (LANES, BLOCK), 0)
    for b in range(tokens // BLOCK):
        kext[HD:, b * BLOCK:(b + 1) * BLOCK] = jnp.where(sub == b, 1.0, 0.0).astype(jnp.bfloat16)
    vext[:, HD:] = jnp.ones((tokens, LANES), jnp.bfloat16)
    listed = b_ref[...]
    block_row = lax.broadcasted_iota(jnp.int32, (tokens // BLOCK, row_count), 0)
    hit = block_row == listed[0:1, :]
    for i in range(1, listed.shape[0]):
        hit = hit | (block_row == listed[i:i + 1, :])
    bias = jnp.where(hit, 0.0, NEG)
    unused = jnp.zeros((LANES - tokens // BLOCK, row_count), jnp.float32)
    mask[...] = jnp.transpose(jnp.concatenate([bias, unused], axis=0)).astype(jnp.bfloat16)

    diag = (
        lax.broadcasted_iota(jnp.int32, (group_rows, LANES), 0)
        == lax.broadcasted_iota(jnp.int32, (group_rows, LANES), 1)
    )
    pad_row = lax.broadcasted_iota(jnp.int32, (PAD, LANES), 0)
    load_k.wait()
    for b in range(tokens // BLOCK):
        at = slice(b * BLOCK, (b + 1) * BLOCK)
        kext[0:HD, at] = jnp.transpose(kbuf[at, :].astype(jnp.float32)).astype(jnp.bfloat16)
    load_v.wait()
    pl.semaphore_wait(ready, ng - 1)

    to_row = lax.broadcasted_iota(jnp.int32, (ng * message, group_rows + PAD), 0)
    from_row = lax.broadcasted_iota(jnp.int32, (ng * message, group_rows + PAD), 1)
    place = to_row % message
    wanted = (place // out_rows) * own_rows + (to_row // message) * out_rows + place % out_rows
    wanted = jnp.where(place < piece_rows, wanted, place - piece_rows + group_rows)
    wanted = jnp.where(place < piece_rows + 3, wanted, -1)
    order = jnp.where(from_row == wanted, 1.0, 0.0).astype(jnp.bfloat16)

    turns = n // SLOTS_PER_TURN

    def turn(step, carry):
        t = (step + 1) % turns
        pieces = []
        for u in range(SLOTS_PER_TURN):
            k = t * SLOTS_PER_TURN + u

            @pl.when(k > 0)
            def _():
                query_copy(k).wait_recv()

            owner = xor(me, k, n)
            bias = mask[pl.ds(pl.multiple_of(owner * own_rows, own_rows), own_rows), :]
            rows = qbuf[k]
            for h in range(QPK):
                pieces.append(jnp.concatenate([rows[:, h * HD:(h + 1) * HD], bias], axis=1))
        query = jnp.concatenate(pieces, axis=0)
        top = None
        for c in range(0, tokens, CHUNK):
            s = jnp.dot(query, kext[:, c:c + CHUNK], preferred_element_type=jnp.float32)
            score[:, c:c + CHUNK] = s
            for i in range(0, CHUNK, LANES):
                part = s[:, i:i + LANES]
                top = part if top is None else jnp.maximum(top, part)
        top = jnp.max(top, axis=1, keepdims=True)
        total = None
        for c in range(0, tokens, CHUNK):
            w = jnp.exp((score[:, c:c + CHUNK] - top) * scale).astype(jnp.bfloat16)
            piece = jnp.dot(w, vext[c:c + CHUNK, :], preferred_element_type=jnp.float32)
            total = piece if total is None else total + piece
        weight = total[:, HD:]
        part = (total[:, :HD] / weight).astype(jnp.bfloat16)
        lse = top * scale + jnp.log(weight)
        for u in range(SLOTS_PER_TURN):
            k = t * SLOTS_PER_TURN + u
            at = slice(u * group_rows, (u + 1) * group_rows)
            line = jnp.sum(jnp.where(diag, lse[at], 0.0), axis=0, keepdims=True)
            high = line.astype(jnp.bfloat16).astype(jnp.float32)
            mid = (line - high).astype(jnp.bfloat16).astype(jnp.float32)
            low = line - high - mid
            tail = jnp.where(pad_row == 0, high, jnp.where(pad_row == 1, mid, jnp.where(pad_row == 2, low, 0.0)))
            block = jnp.concatenate([part[at], tail.astype(jnp.bfloat16)], axis=0)
            part_out[k] = jnp.dot(order, block, preferred_element_type=jnp.float32).astype(jnp.bfloat16)
            for j in range(1, ng):
                part_copy(k, j).start()

            @pl.when(k > 0)
            def _():
                part_copy(k, 0).start()

        return carry

    lax.fori_loop(0, turns, turn, 0)

    part_in[0, 0] = part_out[0, pl.ds(pl.multiple_of(grp * message, PAD), message), :]
    width = QPK * HD
    for j in range(ng):
        for k in range(n):
            if (k, j) != (0, 0):
                part_copy(k, j).wait_recv()
        lines = [
            jnp.sum(part_in[k, j, piece_rows:, :].astype(jnp.float32), axis=0, keepdims=True) for k in range(n)
        ]
        best = functools.reduce(jnp.maximum, lines)
        factors = [jnp.exp(x - best) for x in lines]
        denominator = sum(factors[1:], factors[0])
        factors.append(jnp.zeros((LANES - n, LANES), jnp.float32))
        columns = jnp.transpose(jnp.concatenate(factors, axis=0) / denominator)
        picks = []
        for h in range(QPK):
            rows = columns[h * own_rows:(h + 1) * own_rows]
            mine = rows[0:out_rows]
            for g in range(1, ng):
                mine = jnp.where(grp == g, rows[g * out_rows:(g + 1) * out_rows], mine)
            picks.append(mine)
        columns = jnp.concatenate(picks, axis=0)
        result = None
        for k in range(n):
            piece = part_in[k, j].astype(jnp.float32)[0:piece_rows] * columns[:, k:k + 1]
            result = piece if result is None else result + piece
        origin = xor(grp, j, ng)
        result = jnp.concatenate([result[h * out_rows:(h + 1) * out_rows] for h in range(QPK)], axis=1)
        o_ref[:, pl.ds(pl.multiple_of(origin * width, LANES), width)] = result.astype(jnp.bfloat16)

    for k in range(n):
        if k > 0:
            query_copy(k).wait_send()
        for j in range(ng):
            if (k, j) != (0, 0):
                part_copy(k, j).wait_send()


def per_device(n, ng, query, keys, values, blocks):
    own_rows, width = query.shape
    tokens = keys.shape[0]
    rows = blocks.shape[0]
    message = -(-(QPK * (own_rows // ng) + 3) // PAD) * PAD
    any_spec = pl.BlockSpec(memory_space=pl.ANY)
    vmem_spec = pl.BlockSpec(memory_space=pltpu.VMEM)
    return pl.pallas_call(
        functools.partial(kernel, n, ng),
        out_shape=jax.ShapeDtypeStruct((own_rows // ng, width * ng), jnp.bfloat16),
        in_specs=[any_spec, any_spec, any_spec, vmem_spec],
        out_specs=vmem_spec,
        scratch_shapes=[
            pltpu.VMEM((n, own_rows, width), jnp.bfloat16),
            pltpu.VMEM((tokens, HD), jnp.bfloat16),
            pltpu.VMEM((2 * HD, tokens), jnp.bfloat16),
            pltpu.VMEM((tokens, 2 * HD), jnp.bfloat16),
            pltpu.VMEM((rows, LANES), jnp.bfloat16),
            pltpu.VMEM((SLOTS_PER_TURN * QPK * own_rows, tokens), jnp.float32),
            pltpu.VMEM((n, ng * message, HD), jnp.bfloat16),
            pltpu.VMEM((n, ng, message, HD), jnp.bfloat16),
            pltpu.SemaphoreType.DMA((3,)),
            pltpu.SemaphoreType.DMA((n,)),
            pltpu.SemaphoreType.DMA((n,)),
            pltpu.SemaphoreType.DMA((n, ng)),
            pltpu.SemaphoreType.DMA((n, ng)),
            pltpu.SemaphoreType.REGULAR,
        ],
        compiler_params=pltpu.CompilerParams(
            collective_id=0, has_side_effects=True, vmem_limit_bytes=60 * 1024 * 1024
        ),
    )(query, keys, values, jnp.transpose(blocks, (1, 2, 0))[0])


def solution(mesh):
    placed = (P("ctx", "grp"), P("ctx", "grp"), P("ctx", "grp"), P(None, "ctx", None))
    body = functools.partial(per_device, mesh.shape["ctx"], mesh.shape["grp"])
    return jax.shard_map(
        body, mesh=mesh, in_specs=placed, out_specs=P(("ctx", "grp"), None), check_vma=False
    )
```

```python
import functools
import math

import jax
import jax.numpy as jnp
from jax import lax
from jax.experimental import pallas as pl
from jax.experimental.pallas import tpu as pltpu
from jax.sharding import PartitionSpec as P

HD = 128
QPK = 5
BLOCK = 128
LANES = 128
NEG = -1e30
PAD = 16
SLOTS_PER_TURN = 4
CHUNK = 1024
MESH = pl.DeviceIdType.MESH


def xor(a, b, n):
    total, bit = 0, 1
    while bit < n:
        total = total + bit * ((a // bit + b // bit) % 2)
        bit *= 2
    return total


def kernel(
    n, ng, q_ref, k_ref, v_ref, b_ref, o_ref,
    qbuf, kbuf, kext, vext, mask, score, part_out, part_in,
    local_sem, qsend, qrecv, psend, precv, ready,
):
    me = lax.axis_index("ctx")
    grp = lax.axis_index("grp")
    own_rows = qbuf.shape[1]
    group_rows = QPK * own_rows
    tokens = kbuf.shape[0]
    message = part_in.shape[2]
    out_rows = own_rows // ng
    piece_rows = QPK * out_rows
    row_count = mask.shape[0]
    scale = 1.0 / math.sqrt(HD)

    barrier = pltpu.get_barrier_semaphore()
    for k in range(1, n):
        pl.semaphore_signal(barrier, inc=1, device_id={"ctx": xor(me, k, n)}, device_id_type=MESH)
    for j in range(1, ng):
        pl.semaphore_signal(barrier, inc=1, device_id={"grp": xor(grp, j, ng)}, device_id_type=MESH)

    load_q = pltpu.make_async_copy(q_ref, qbuf.at[0], local_sem.at[0])
    load_k = pltpu.make_async_copy(k_ref, kbuf, local_sem.at[1])
    load_v = pltpu.make_async_copy(v_ref, vext.at[:, 0:HD], local_sem.at[2])
    load_q.start()
    load_k.start()
    load_v.start()

    def query_copy(k):
        return pltpu.make_async_remote_copy(
            src_ref=qbuf.at[0], dst_ref=qbuf.at[k], send_sem=qsend.at[k], recv_sem=qrecv.at[k],
            device_id={"ctx": xor(me, k, n)}, device_id_type=MESH,
        )

    def part_copy(k, j):
        target = xor(grp, j, ng)
        return pltpu.make_async_remote_copy(
            src_ref=part_out.at[k, pl.ds(pl.multiple_of(target * message, PAD), message)],
            dst_ref=part_in.at[k, j], send_sem=psend.at[k, j], recv_sem=precv.at[k, j],
            device_id={"ctx": xor(me, k, n), "grp": target}, device_id_type=MESH,
        )

    pl.semaphore_wait(barrier, n - 1 + ng - 1)
    for j in range(1, ng):
        pl.semaphore_signal(ready, inc=1, device_id={"grp": xor(grp, j, ng)}, device_id_type=MESH)
    load_q.wait()
    for k in range(1, n):
        query_copy(k).start()

    sub = lax.broadcasted_iota(jnp.int32, (LANES, BLOCK), 0)
    for b in range(tokens // BLOCK):
        kext[HD:, b * BLOCK:(b + 1) * BLOCK] = jnp.where(sub == b, 1.0, 0.0).astype(jnp.bfloat16)
    vext[:, HD:] = jnp.ones((tokens, LANES), jnp.bfloat16)
    listed = b_ref[...]
    block_row = lax.broadcasted_iota(jnp.int32, (tokens // BLOCK, row_count), 0)
    hit = block_row == listed[0:1, :]
    for i in range(1, listed.shape[0]):
        hit = hit | (block_row == listed[i:i + 1, :])
    bias = jnp.where(hit, 0.0, NEG)
    unused = jnp.zeros((LANES - tokens // BLOCK, row_count), jnp.float32)
    mask[...] = jnp.transpose(jnp.concatenate([bias, unused], axis=0)).astype(jnp.bfloat16)

    diag = (
        lax.broadcasted_iota(jnp.int32, (group_rows, LANES), 0)
        == lax.broadcasted_iota(jnp.int32, (group_rows, LANES), 1)
    )
    pad_row = lax.broadcasted_iota(jnp.int32, (PAD, LANES), 0)
    load_k.wait()
    for b in range(tokens // BLOCK):
        at = slice(b * BLOCK, (b + 1) * BLOCK)
        kext[0:HD, at] = jnp.transpose(kbuf[at, :].astype(jnp.float32)).astype(jnp.bfloat16)
    load_v.wait()
    pl.semaphore_wait(ready, ng - 1)

    to_row = lax.broadcasted_iota(jnp.int32, (ng * message, group_rows + PAD), 0)
    from_row = lax.broadcasted_iota(jnp.int32, (ng * message, group_rows + PAD), 1)
    place = to_row % message
    wanted = (place // out_rows) * own_rows + (to_row // message) * out_rows + place % out_rows
    wanted = jnp.where(place < piece_rows, wanted, place - piece_rows + group_rows)
    wanted = jnp.where(place < piece_rows + 3, wanted, -1)
    order = jnp.where(from_row == wanted, 1.0, 0.0).astype(jnp.bfloat16)

    turns = n // SLOTS_PER_TURN

    def turn(step, carry):
        t = (step + 1) % turns
        pieces = []
        for u in range(SLOTS_PER_TURN):
            k = t * SLOTS_PER_TURN + u

            @pl.when(k > 0)
            def _():
                query_copy(k).wait_recv()

            owner = xor(me, k, n)
            bias = mask[pl.ds(pl.multiple_of(owner * own_rows, own_rows), own_rows), :]
            rows = qbuf[k]
            for h in range(QPK):
                pieces.append(jnp.concatenate([rows[:, h * HD:(h + 1) * HD], bias], axis=1))
        query = jnp.concatenate(pieces, axis=0)
        top = None
        for c in range(0, tokens, CHUNK):
            s = jnp.dot(query, kext[:, c:c + CHUNK], preferred_element_type=jnp.float32)
            score[:, c:c + CHUNK] = s
            for i in range(0, CHUNK, LANES):
                part = s[:, i:i + LANES]
                top = part if top is None else jnp.maximum(top, part)
        top = jnp.max(top, axis=1, keepdims=True)
        total = None
        for c in range(0, tokens, CHUNK):
            w = jnp.exp((score[:, c:c + CHUNK] - top) * scale).astype(jnp.bfloat16)
            piece = jnp.dot(w, vext[c:c + CHUNK, :], preferred_element_type=jnp.float32)
            total = piece if total is None else total + piece
        weight = total[:, HD:]
        part = (total[:, :HD] / weight).astype(jnp.bfloat16)
        lse = top * scale + jnp.log(weight)
        for u in range(SLOTS_PER_TURN):
            k = t * SLOTS_PER_TURN + u
            at = slice(u * group_rows, (u + 1) * group_rows)
            line = jnp.sum(jnp.where(diag, lse[at], 0.0), axis=0, keepdims=True)
            high = line.astype(jnp.bfloat16).astype(jnp.float32)
            mid = (line - high).astype(jnp.bfloat16).astype(jnp.float32)
            low = line - high - mid
            tail = jnp.where(pad_row == 0, high, jnp.where(pad_row == 1, mid, jnp.where(pad_row == 2, low, 0.0)))
            block = jnp.concatenate([part[at], tail.astype(jnp.bfloat16)], axis=0)
            part_out[k] = jnp.dot(order, block, preferred_element_type=jnp.float32).astype(jnp.bfloat16)
            for j in range(1, ng):
                part_copy(k, j).start()

            @pl.when(k > 0)
            def _():
                part_copy(k, 0).start()

        return carry

    lax.fori_loop(0, turns, turn, 0)

    part_in[0, 0] = part_out[0, pl.ds(pl.multiple_of(grp * message, PAD), message), :]
    width = QPK * HD
    for j in range(ng):
        for k in range(n):
            if (k, j) != (0, 0):
                part_copy(k, j).wait_recv()
        lines = [
            jnp.sum(part_in[k, j, piece_rows:, :].astype(jnp.float32), axis=0, keepdims=True) for k in range(n)
        ]
        best = functools.reduce(jnp.maximum, lines)
        factors = [jnp.exp(x - best) for x in lines]
        denominator = sum(factors[1:], factors[0])
        factors.append(jnp.zeros((LANES - n, LANES), jnp.float32))
        columns = jnp.transpose(jnp.concatenate(factors, axis=0) / denominator)
        picks = []
        for h in range(QPK):
            rows = columns[h * own_rows:(h + 1) * own_rows]
            mine = rows[0:out_rows]
            for g in range(1, ng):
                mine = jnp.where(grp == g, rows[g * out_rows:(g + 1) * out_rows], mine)
            picks.append(mine)
        columns = jnp.concatenate(picks, axis=0)
        result = None
        for k in range(n):
            piece = part_in[k, j].astype(jnp.float32)[0:piece_rows] * columns[:, k:k + 1]
            result = piece if result is None else result + piece
        origin = xor(grp, j, ng)
        result = jnp.concatenate([result[h * out_rows:(h + 1) * out_rows] for h in range(QPK)], axis=1)
        o_ref[:, pl.ds(pl.multiple_of(origin * width, LANES), width)] = result.astype(jnp.bfloat16)

    for k in range(n):
        if k > 0:
            query_copy(k).wait_send()
        for j in range(ng):
            if (k, j) != (0, 0):
                part_copy(k, j).wait_send()


def per_device(n, ng, query, keys, values, blocks):
    own_rows, width = query.shape
    tokens = keys.shape[0]
    rows = blocks.shape[0]
    message = -(-(QPK * (own_rows // ng) + 3) // PAD) * PAD
    any_spec = pl.BlockSpec(memory_space=pl.ANY)
    vmem_spec = pl.BlockSpec(memory_space=pltpu.VMEM)
    return pl.pallas_call(
        functools.partial(kernel, n, ng),
        out_shape=jax.ShapeDtypeStruct((own_rows // ng, width * ng), jnp.bfloat16),
        in_specs=[any_spec, any_spec, any_spec, vmem_spec],
        out_specs=vmem_spec,
        scratch_shapes=[
            pltpu.VMEM((n, own_rows, width), jnp.bfloat16),
            pltpu.VMEM((tokens, HD), jnp.bfloat16),
            pltpu.VMEM((2 * HD, tokens), jnp.bfloat16),
            pltpu.VMEM((tokens, 2 * HD), jnp.bfloat16),
            pltpu.VMEM((rows, LANES), jnp.bfloat16),
            pltpu.VMEM((SLOTS_PER_TURN * QPK * own_rows, tokens), jnp.float32),
            pltpu.VMEM((n, ng * message, HD), jnp.bfloat16),
            pltpu.VMEM((n, ng, message, HD), jnp.bfloat16),
            pltpu.SemaphoreType.DMA((3,)),
            pltpu.SemaphoreType.DMA((n,)),
            pltpu.SemaphoreType.DMA((n,)),
            pltpu.SemaphoreType.DMA((n, ng)),
            pltpu.SemaphoreType.DMA((n, ng)),
            pltpu.SemaphoreType.REGULAR,
        ],
        compiler_params=pltpu.CompilerParams(
            collective_id=0, has_side_effects=True, vmem_limit_bytes=60 * 1024 * 1024
        ),
    )(query, keys, values, jnp.transpose(blocks, (1, 2, 0))[0])


def solution(mesh):
    placed = (P("ctx", "grp"), P("ctx", "grp"), P("ctx", "grp"), P(None, "ctx", None))
    body = functools.partial(per_device, mesh.shape["ctx"], mesh.shape["grp"])
    return jax.shard_map(
        body, mesh=mesh, in_specs=placed, out_specs=P(("ctx", "grp"), None), check_vma=False
    )
```

```python
import functools
import math

import jax
import jax.numpy as jnp
from jax import lax
from jax.experimental import pallas as pl
from jax.experimental.pallas import tpu as pltpu
from jax.sharding import PartitionSpec as P

HD = 128
QPK = 5
BLOCK = 128
LANES = 128
NEG = -1e30
PAD = 16
SLOTS_PER_TURN = 2
CHUNK = 1024
LOADS = 4
UNROLL = 4
MESH = pl.DeviceIdType.MESH


def bits_of(a, n):
    bits, bit = [], 1
    while bit < n:
        bits.append(lax.rem(lax.div(a, bit), 2) if not isinstance(a, int) else (a // bit) % 2)
        bit *= 2
    return bits


def xor(a_bits, b, n):
    total = 0
    for i, (x, y) in enumerate(zip(a_bits, bits_of(b, n))):
        if isinstance(y, int):
            total = total + (1 << i) * (1 - x if y else x)
        else:
            total = total + (1 << i) * (x + y - 2 * x * y)
    return total


def kernel(
    n, ng, q_ref, k_ref, v_ref, b_ref, o_ref,
    lists, qbuf, kbuf, kext, vext, mask, score, part_out, part_in,
    local_sem, qsend, qrecv, psend, precv, ready,
):
    me = lax.axis_index("ctx")
    grp = lax.axis_index("grp")
    me_bits, grp_bits = bits_of(me, n), bits_of(grp, ng)
    targets = [xor(grp_bits, j, ng) for j in range(ng)]
    own_rows = qbuf.shape[1]
    group_rows = QPK * own_rows
    tokens = kbuf.shape[0]
    message = part_in.shape[2]
    out_rows = own_rows // ng
    piece_rows = QPK * out_rows
    row_count = mask.shape[0]
    scale = 1.0 / math.sqrt(HD)

    barrier = pltpu.get_barrier_semaphore()
    for k in range(1, n):
        pl.semaphore_signal(barrier, inc=1, device_id={"ctx": xor(me_bits, k, n)}, device_id_type=MESH)
    for j in range(1, ng):
        pl.semaphore_signal(barrier, inc=1, device_id={"grp": targets[j]}, device_id_type=MESH)

    load_q = pltpu.make_async_copy(q_ref, qbuf.at[0], local_sem.at[0])
    load_b = pltpu.make_async_copy(b_ref, lists, local_sem.at[1])
    load_q.start()
    load_b.start()
    part_tokens = tokens // LOADS
    load_k, load_v = [], []
    for i in range(LOADS):
        at = slice(i * part_tokens, (i + 1) * part_tokens)
        load_k.append(pltpu.make_async_copy(k_ref.at[at], kbuf.at[at], local_sem.at[2 + i]))
        load_v.append(pltpu.make_async_copy(v_ref.at[at], vext.at[at, 0:HD], local_sem.at[2 + LOADS + i]))
    for copy in load_k + load_v:
        copy.start()

    def query_copy(k):
        return pltpu.make_async_remote_copy(
            src_ref=qbuf.at[0], dst_ref=qbuf.at[k], send_sem=qsend.at[k], recv_sem=qrecv.at[k],
            device_id={"ctx": xor(me_bits, k, n)}, device_id_type=MESH,
        )

    def part_copy(k, j):
        target = targets[j]
        return pltpu.make_async_remote_copy(
            src_ref=part_out.at[k, pl.ds(pl.multiple_of(target * message, PAD), message)],
            dst_ref=part_in.at[k, j], send_sem=psend.at[k, j], recv_sem=precv.at[k, j],
            device_id={"ctx": xor(me_bits, k, n), "grp": target}, device_id_type=MESH,
        )

    sub = lax.broadcasted_iota(jnp.int32, (LANES, BLOCK), 0)
    for b in range(tokens // BLOCK):
        kext[HD:, b * BLOCK:(b + 1) * BLOCK] = jnp.where(sub == b, 1.0, 0.0).astype(jnp.bfloat16)
    vext[:, HD:] = jnp.ones((tokens, LANES), jnp.bfloat16)
    diag = (
        lax.broadcasted_iota(jnp.int32, (group_rows, LANES), 0)
        == lax.broadcasted_iota(jnp.int32, (group_rows, LANES), 1)
    )
    pad_row = lax.broadcasted_iota(jnp.int32, (PAD, LANES), 0)

    to_row = lax.broadcasted_iota(jnp.int32, (ng * message, group_rows + PAD), 0)
    from_row = lax.broadcasted_iota(jnp.int32, (ng * message, group_rows + PAD), 1)
    message_bits, piece_bits = message.bit_length() - 1, out_rows.bit_length() - 1
    place = to_row & (message - 1)
    wanted = (place >> piece_bits) * own_rows + (to_row >> message_bits) * out_rows + (place & (out_rows - 1))
    wanted = jnp.where(place < piece_rows, wanted, place - piece_rows + group_rows)
    wanted = jnp.where(place < piece_rows + 3, wanted, -1)
    order = jnp.where(from_row == wanted, 1.0, 0.0).astype(jnp.bfloat16)

    pl.semaphore_wait(barrier, n - 1 + ng - 1)
    for j in range(1, ng):
        pl.semaphore_signal(ready, inc=1, device_id={"grp": targets[j]}, device_id_type=MESH)
    load_q.wait()
    for k in range(1, n):
        query_copy(k).start()

    load_b.wait()
    listed = lists[...]
    block_row = lax.broadcasted_iota(jnp.int32, (tokens // BLOCK, row_count), 0)
    hit = block_row == listed[0:1, :]
    for i in range(1, listed.shape[0]):
        hit = hit | (block_row == listed[i:i + 1, :])
    bias = jnp.where(hit, 0.0, NEG)
    unused = jnp.zeros((LANES - tokens // BLOCK, row_count), jnp.float32)
    mask[...] = jnp.transpose(jnp.concatenate([bias, unused], axis=0)).astype(jnp.bfloat16)

    for i in range(LOADS):
        load_k[i].wait()
        for c in range(i * part_tokens, (i + 1) * part_tokens, BLOCK):
            at = slice(c, c + BLOCK)
            kext[0:HD, at] = jnp.transpose(kbuf[at, :].astype(jnp.float32)).astype(jnp.bfloat16)
    for copy in load_v:
        copy.wait()
    pl.semaphore_wait(ready, ng - 1)

    turns = n // SLOTS_PER_TURN

    def turn(step, carry):
        t = (step + 1) % turns if isinstance(step, int) else lax.rem(step + 1, turns)
        pieces = []
        for u in range(SLOTS_PER_TURN):
            k = t * SLOTS_PER_TURN + u

            if isinstance(k, int):
                if k > 0:
                    query_copy(k).wait_recv()
            else:
                pl.when(k > 0)(lambda: query_copy(k).wait_recv())

            owner = xor(me_bits, k, n)
            bias = mask[pl.ds(pl.multiple_of(owner * own_rows, own_rows), own_rows), :]
            rows = qbuf[k]
            for h in range(QPK):
                pieces.append(jnp.concatenate([rows[:, h * HD:(h + 1) * HD], bias], axis=1))
        query = jnp.concatenate(pieces, axis=0)
        top = None
        for c in range(0, tokens, CHUNK):
            s = jnp.dot(query, kext[:, c:c + CHUNK], preferred_element_type=jnp.float32)
            score[:, c:c + CHUNK] = s
            for i in range(0, CHUNK, LANES):
                part = s[:, i:i + LANES]
                top = part if top is None else jnp.maximum(top, part)
        top = jnp.max(top, axis=1, keepdims=True)
        total = None
        for c in range(0, tokens, CHUNK):
            w = jnp.exp((score[:, c:c + CHUNK] - top) * scale).astype(jnp.bfloat16)
            piece = jnp.dot(w, vext[c:c + CHUNK, :], preferred_element_type=jnp.float32)
            total = piece if total is None else total + piece
        weight = total[:, HD:]
        part = (total[:, :HD] / weight).astype(jnp.bfloat16)
        lse = top * scale + jnp.log(weight)
        for u in range(SLOTS_PER_TURN):
            k = t * SLOTS_PER_TURN + u
            at = slice(u * group_rows, (u + 1) * group_rows)
            line = jnp.sum(jnp.where(diag, lse[at], 0.0), axis=0, keepdims=True)
            high = line.astype(jnp.bfloat16).astype(jnp.float32)
            mid = (line - high).astype(jnp.bfloat16).astype(jnp.float32)
            low = line - high - mid
            tail = jnp.where(pad_row == 0, high, jnp.where(pad_row == 1, mid, jnp.where(pad_row == 2, low, 0.0)))
            block = jnp.concatenate([part[at], tail.astype(jnp.bfloat16)], axis=0)
            part_out[k] = jnp.dot(order, block, preferred_element_type=jnp.float32).astype(jnp.bfloat16)
            for j in range(1, ng):
                part_copy(k, j).start()

            if isinstance(k, int):
                if k > 0:
                    part_copy(k, 0).start()
            else:
                pl.when(k > 0)(lambda: part_copy(k, 0).start())

        return carry

    if turns <= UNROLL:
        for step in range(turns):
            turn(step, 0)
    else:
        lax.fori_loop(0, turns, turn, 0)

    part_in[0, 0] = part_out[0, pl.ds(pl.multiple_of(grp * message, PAD), message), :]
    width = QPK * HD
    for j in range(ng):
        for k in range(n):
            if (k, j) != (0, 0):
                part_copy(k, j).wait_recv()
        lines = [
            jnp.sum(part_in[k, j, piece_rows:, :].astype(jnp.float32), axis=0, keepdims=True) for k in range(n)
        ]
        best = functools.reduce(jnp.maximum, lines)
        factors = [jnp.exp(x - best) for x in lines]
        denominator = sum(factors[1:], factors[0])
        factors.append(jnp.zeros((LANES - n, LANES), jnp.float32))
        columns = jnp.transpose(jnp.concatenate(factors, axis=0) / denominator)
        picks = []
        for h in range(QPK):
            rows = columns[h * own_rows:(h + 1) * own_rows]
            mine = rows[0:out_rows]
            for g in range(1, ng):
                mine = jnp.where(grp == g, rows[g * out_rows:(g + 1) * out_rows], mine)
            picks.append(mine)
        columns = jnp.concatenate(picks, axis=0)
        result = None
        for k in range(n):
            piece = part_in[k, j].astype(jnp.float32)[0:piece_rows] * columns[:, k:k + 1]
            result = piece if result is None else result + piece
        origin = targets[j]
        result = jnp.concatenate([result[h * out_rows:(h + 1) * out_rows] for h in range(QPK)], axis=1)
        o_ref[:, pl.ds(pl.multiple_of(origin * width, LANES), width)] = result.astype(jnp.bfloat16)

    for k in range(n):
        if k > 0:
            query_copy(k).wait_send()
        for j in range(ng):
            if (k, j) != (0, 0):
                part_copy(k, j).wait_send()


def per_device(n, ng, query, keys, values, blocks):
    own_rows, width = query.shape
    tokens = keys.shape[0]
    rows = blocks.shape[0]
    message = -(-(QPK * (own_rows // ng) + 3) // PAD) * PAD
    any_spec = pl.BlockSpec(memory_space=pl.ANY)
    vmem_spec = pl.BlockSpec(memory_space=pltpu.VMEM)
    return pl.pallas_call(
        functools.partial(kernel, n, ng),
        out_shape=jax.ShapeDtypeStruct((own_rows // ng, width * ng), jnp.bfloat16),
        in_specs=[any_spec] * 4,
        out_specs=vmem_spec,
        scratch_shapes=[
            pltpu.VMEM((blocks.shape[2], rows), jnp.int32),
            pltpu.VMEM((n, own_rows, width), jnp.bfloat16),
            pltpu.VMEM((tokens, HD), jnp.bfloat16),
            pltpu.VMEM((2 * HD, tokens), jnp.bfloat16),
            pltpu.VMEM((tokens, 2 * HD), jnp.bfloat16),
            pltpu.VMEM((rows, LANES), jnp.bfloat16),
            pltpu.VMEM((SLOTS_PER_TURN * QPK * own_rows, tokens), jnp.float32),
            pltpu.VMEM((n, ng * message, HD), jnp.bfloat16),
            pltpu.VMEM((n, ng, message, HD), jnp.bfloat16),
            pltpu.SemaphoreType.DMA((2 + 2 * LOADS,)),
            pltpu.SemaphoreType.DMA((n,)),
            pltpu.SemaphoreType.DMA((n,)),
            pltpu.SemaphoreType.DMA((n, ng)),
            pltpu.SemaphoreType.DMA((n, ng)),
            pltpu.SemaphoreType.REGULAR,
        ],
        compiler_params=pltpu.CompilerParams(
            collective_id=0, has_side_effects=True, vmem_limit_bytes=60 * 1024 * 1024
        ),
    )(query, keys, values, jnp.transpose(blocks, (1, 2, 0))[0])


def solution(mesh):
    placed = (P("ctx", "grp"), P("ctx", "grp"), P("ctx", "grp"), P(None, "ctx", None))
    body = functools.partial(per_device, mesh.shape["ctx"], mesh.shape["grp"])
    return jax.shard_map(
        body, mesh=mesh, in_specs=placed, out_specs=P(("ctx", "grp"), None), check_vma=False
    )
```

```python
import functools
import math

import jax
import jax.numpy as jnp
from jax import lax
from jax.experimental import pallas as pl
from jax.experimental.pallas import tpu as pltpu
from jax.sharding import PartitionSpec as P

HD = 128
QPK = 5
BLOCK = 128
LANES = 128
NEG = -1e30
PAD = 16
SLOTS_PER_TURN = 2
CHUNK = 1024
LOADS = 4
UNROLL = 4
MESH = pl.DeviceIdType.MESH


def bits_of(a, n):
    bits, bit = [], 1
    while bit < n:
        bits.append(lax.rem(lax.div(a, bit), 2) if not isinstance(a, int) else (a // bit) % 2)
        bit *= 2
    return bits


def xor(a_bits, b, n):
    total = 0
    for i, (x, y) in enumerate(zip(a_bits, bits_of(b, n))):
        if isinstance(y, int):
            total = total + (1 << i) * (1 - x if y else x)
        else:
            total = total + (1 << i) * (x + y - 2 * x * y)
    return total


def kernel(
    n, ng, q_ref, k_ref, v_ref, b_ref, o_ref,
    lists, qbuf, kbuf, kext, vext, mask, score, part_out, part_in,
    local_sem, qsend, qrecv, psend, precv, ready,
):
    me = lax.axis_index("ctx")
    grp = lax.axis_index("grp")
    me_bits, grp_bits = bits_of(me, n), bits_of(grp, ng)
    targets = [xor(grp_bits, j, ng) for j in range(ng)]
    own_rows = qbuf.shape[1]
    group_rows = QPK * own_rows
    tokens = kbuf.shape[0]
    message = part_in.shape[2]
    out_rows = own_rows // ng
    piece_rows = QPK * out_rows
    row_count = mask.shape[0]
    scale = 1.0 / math.sqrt(HD)

    barrier = pltpu.get_barrier_semaphore()
    for k in range(1, n):
        pl.semaphore_signal(barrier, inc=1, device_id={"ctx": xor(me_bits, k, n)}, device_id_type=MESH)
    for j in range(1, ng):
        pl.semaphore_signal(barrier, inc=1, device_id={"grp": targets[j]}, device_id_type=MESH)

    load_q = pltpu.make_async_copy(q_ref, qbuf.at[0], local_sem.at[0])
    load_b = pltpu.make_async_copy(b_ref, lists, local_sem.at[1])
    load_q.start()
    load_b.start()
    part_tokens = tokens // LOADS
    load_k, load_v = [], []
    for i in range(LOADS):
        at = slice(i * part_tokens, (i + 1) * part_tokens)
        load_k.append(pltpu.make_async_copy(k_ref.at[at], kbuf.at[at], local_sem.at[2 + i]))
        load_v.append(pltpu.make_async_copy(v_ref.at[at], vext.at[at, 0:HD], local_sem.at[2 + LOADS + i]))
    for copy in load_k + load_v:
        copy.start()

    def query_copy(k):
        return pltpu.make_async_remote_copy(
            src_ref=qbuf.at[0], dst_ref=qbuf.at[k], send_sem=qsend.at[k], recv_sem=qrecv.at[k],
            device_id={"ctx": xor(me_bits, k, n)}, device_id_type=MESH,
        )

    def part_copy(k, j):
        target = targets[j]
        return pltpu.make_async_remote_copy(
            src_ref=part_out.at[k, pl.ds(pl.multiple_of(target * message, PAD), message)],
            dst_ref=part_in.at[k, j], send_sem=psend.at[k, j], recv_sem=precv.at[k, j],
            device_id={"ctx": xor(me_bits, k, n), "grp": target}, device_id_type=MESH,
        )

    sub = lax.broadcasted_iota(jnp.int32, (LANES, BLOCK), 0)
    for b in range(tokens // BLOCK):
        kext[HD:, b * BLOCK:(b + 1) * BLOCK] = jnp.where(sub == b, 1.0, 0.0).astype(jnp.bfloat16)
    vext[:, HD:] = jnp.ones((tokens, LANES), jnp.bfloat16)
    diag = (
        lax.broadcasted_iota(jnp.int32, (group_rows, LANES), 0)
        == lax.broadcasted_iota(jnp.int32, (group_rows, LANES), 1)
    )
    pad_row = lax.broadcasted_iota(jnp.int32, (PAD, LANES), 0)

    to_row = lax.broadcasted_iota(jnp.int32, (ng * message, group_rows + PAD), 0)
    from_row = lax.broadcasted_iota(jnp.int32, (ng * message, group_rows + PAD), 1)
    message_bits, piece_bits = message.bit_length() - 1, out_rows.bit_length() - 1
    place = to_row & (message - 1)
    wanted = (place >> piece_bits) * own_rows + (to_row >> message_bits) * out_rows + (place & (out_rows - 1))
    wanted = jnp.where(place < piece_rows, wanted, place - piece_rows + group_rows)
    wanted = jnp.where(place < piece_rows + 3, wanted, -1)
    order = jnp.where(from_row == wanted, 1.0, 0.0).astype(jnp.bfloat16)

    pl.semaphore_wait(barrier, n - 1 + ng - 1)
    for j in range(1, ng):
        pl.semaphore_signal(ready, inc=1, device_id={"grp": targets[j]}, device_id_type=MESH)
    load_q.wait()
    for k in range(n - 1, 0, -1):
        query_copy(k).start()

    load_b.wait()
    listed = lists[...]
    block_row = lax.broadcasted_iota(jnp.int32, (tokens // BLOCK, row_count), 0)
    hit = block_row == listed[0:1, :]
    for i in range(1, listed.shape[0]):
        hit = hit | (block_row == listed[i:i + 1, :])
    bias = jnp.where(hit, 0.0, NEG)
    unused = jnp.zeros((LANES - tokens // BLOCK, row_count), jnp.float32)
    mask[...] = jnp.transpose(jnp.concatenate([bias, unused], axis=0)).astype(jnp.bfloat16)

    for i in range(LOADS):
        load_k[i].wait()
        for c in range(i * part_tokens, (i + 1) * part_tokens, BLOCK):
            at = slice(c, c + BLOCK)
            kext[0:HD, at] = jnp.transpose(kbuf[at, :].astype(jnp.float32)).astype(jnp.bfloat16)
    for copy in load_v:
        copy.wait()
    pl.semaphore_wait(ready, ng - 1)

    turns = n // SLOTS_PER_TURN

    def turn(step, carry):
        t = turns - 1 - step
        pieces = []
        for u in range(SLOTS_PER_TURN):
            k = t * SLOTS_PER_TURN + u

            if isinstance(k, int):
                if k > 0:
                    query_copy(k).wait_recv()
            else:
                pl.when(k > 0)(lambda: query_copy(k).wait_recv())

            owner = xor(me_bits, k, n)
            bias = mask[pl.ds(pl.multiple_of(owner * own_rows, own_rows), own_rows), :]
            rows = qbuf[k]
            for h in range(QPK):
                pieces.append(jnp.concatenate([rows[:, h * HD:(h + 1) * HD], bias], axis=1))
        query = jnp.concatenate(pieces, axis=0)
        top = None
        for c in range(0, tokens, CHUNK):
            s = jnp.dot(query, kext[:, c:c + CHUNK], preferred_element_type=jnp.float32)
            score[:, c:c + CHUNK] = s
            for i in range(0, CHUNK, LANES):
                part = s[:, i:i + LANES]
                top = part if top is None else jnp.maximum(top, part)
        top = jnp.max(top, axis=1, keepdims=True)
        total = None
        for c in range(0, tokens, CHUNK):
            w = jnp.exp((score[:, c:c + CHUNK] - top) * scale).astype(jnp.bfloat16)
            piece = jnp.dot(w, vext[c:c + CHUNK, :], preferred_element_type=jnp.float32)
            total = piece if total is None else total + piece
        weight = total[:, HD:]
        part = (total[:, :HD] / weight).astype(jnp.bfloat16)
        lse = top * scale + jnp.log(weight)
        for u in range(SLOTS_PER_TURN):
            k = t * SLOTS_PER_TURN + u
            at = slice(u * group_rows, (u + 1) * group_rows)
            line = jnp.sum(jnp.where(diag, lse[at], 0.0), axis=0, keepdims=True)
            high = line.astype(jnp.bfloat16).astype(jnp.float32)
            mid = (line - high).astype(jnp.bfloat16).astype(jnp.float32)
            low = line - high - mid
            tail = jnp.where(pad_row == 0, high, jnp.where(pad_row == 1, mid, jnp.where(pad_row == 2, low, 0.0)))
            block = jnp.concatenate([part[at], tail.astype(jnp.bfloat16)], axis=0)
            part_out[k] = jnp.dot(order, block, preferred_element_type=jnp.float32).astype(jnp.bfloat16)
            for j in range(1, ng):
                part_copy(k, j).start()

            if isinstance(k, int):
                if k > 0:
                    part_copy(k, 0).start()
            else:
                pl.when(k > 0)(lambda: part_copy(k, 0).start())

        return carry

    if turns <= UNROLL:
        for step in range(turns):
            turn(step, 0)
    else:
        lax.fori_loop(0, turns, turn, 0)

    part_in[0, 0] = part_out[0, pl.ds(pl.multiple_of(grp * message, PAD), message), :]
    width = QPK * HD
    for j in range(ng):
        for k in range(n):
            if (k, j) != (0, 0):
                part_copy(k, j).wait_recv()
        lines = [
            jnp.sum(part_in[k, j, piece_rows:, :].astype(jnp.float32), axis=0, keepdims=True) for k in range(n)
        ]
        best = functools.reduce(jnp.maximum, lines)
        factors = [jnp.exp(x - best) for x in lines]
        denominator = sum(factors[1:], factors[0])
        factors.append(jnp.zeros((LANES - n, LANES), jnp.float32))
        columns = jnp.transpose(jnp.concatenate(factors, axis=0) / denominator)
        picks = []
        for h in range(QPK):
            rows = columns[h * own_rows:(h + 1) * own_rows]
            mine = rows[0:out_rows]
            for g in range(1, ng):
                mine = jnp.where(grp == g, rows[g * out_rows:(g + 1) * out_rows], mine)
            picks.append(mine)
        columns = jnp.concatenate(picks, axis=0)
        result = None
        for k in range(n):
            piece = part_in[k, j].astype(jnp.float32)[0:piece_rows] * columns[:, k:k + 1]
            result = piece if result is None else result + piece
        origin = targets[j]
        result = jnp.concatenate([result[h * out_rows:(h + 1) * out_rows] for h in range(QPK)], axis=1)
        o_ref[:, pl.ds(pl.multiple_of(origin * width, LANES), width)] = result.astype(jnp.bfloat16)

    for k in range(n):
        if k > 0:
            query_copy(k).wait_send()
        for j in range(ng):
            if (k, j) != (0, 0):
                part_copy(k, j).wait_send()


def per_device(n, ng, query, keys, values, blocks):
    own_rows, width = query.shape
    tokens = keys.shape[0]
    rows = blocks.shape[0]
    message = -(-(QPK * (own_rows // ng) + 3) // PAD) * PAD
    any_spec = pl.BlockSpec(memory_space=pl.ANY)
    vmem_spec = pl.BlockSpec(memory_space=pltpu.VMEM)
    return pl.pallas_call(
        functools.partial(kernel, n, ng),
        out_shape=jax.ShapeDtypeStruct((own_rows // ng, width * ng), jnp.bfloat16),
        in_specs=[any_spec] * 4,
        out_specs=vmem_spec,
        scratch_shapes=[
            pltpu.VMEM((blocks.shape[2], rows), jnp.int32),
            pltpu.VMEM((n, own_rows, width), jnp.bfloat16),
            pltpu.VMEM((tokens, HD), jnp.bfloat16),
            pltpu.VMEM((2 * HD, tokens), jnp.bfloat16),
            pltpu.VMEM((tokens, 2 * HD), jnp.bfloat16),
            pltpu.VMEM((rows, LANES), jnp.bfloat16),
            pltpu.VMEM((SLOTS_PER_TURN * QPK * own_rows, tokens), jnp.float32),
            pltpu.VMEM((n, ng * message, HD), jnp.bfloat16),
            pltpu.VMEM((n, ng, message, HD), jnp.bfloat16),
            pltpu.SemaphoreType.DMA((2 + 2 * LOADS,)),
            pltpu.SemaphoreType.DMA((n,)),
            pltpu.SemaphoreType.DMA((n,)),
            pltpu.SemaphoreType.DMA((n, ng)),
            pltpu.SemaphoreType.DMA((n, ng)),
            pltpu.SemaphoreType.REGULAR,
        ],
        compiler_params=pltpu.CompilerParams(
            collective_id=0, has_side_effects=True, vmem_limit_bytes=60 * 1024 * 1024
        ),
    )(query, keys, values, jnp.transpose(blocks, (1, 2, 0))[0])


def solution(mesh):
    placed = (P("ctx", "grp"), P("ctx", "grp"), P("ctx", "grp"), P(None, "ctx", None))
    body = functools.partial(per_device, mesh.shape["ctx"], mesh.shape["grp"])
    return jax.shard_map(
        body, mesh=mesh, in_specs=placed, out_specs=P(("ctx", "grp"), None), check_vma=False
    )
```

```python
import functools
import math

import jax
import jax.numpy as jnp
from jax import lax
from jax.experimental import pallas as pl
from jax.experimental.pallas import tpu as pltpu
from jax.sharding import PartitionSpec as P

HD = 128
QPK = 5
BLOCK = 128
LANES = 128
NEG = -1e30
PAD = 16
SLOTS_PER_TURN = 2
CHUNK = 1024
LOADS = 4
UNROLL = 4
MESH = pl.DeviceIdType.MESH


def bits_of(a, n):
    bits, bit = [], 1
    while bit < n:
        bits.append(lax.rem(lax.div(a, bit), 2) if not isinstance(a, int) else (a // bit) % 2)
        bit *= 2
    return bits


def xor(a_bits, b, n):
    total = 0
    for i, (x, y) in enumerate(zip(a_bits, bits_of(b, n))):
        if isinstance(y, int):
            total = total + (1 << i) * (1 - x if y else x)
        else:
            total = total + (1 << i) * (x + y - 2 * x * y)
    return total


def kernel(
    n, ng, q_ref, k_ref, v_ref, b_ref, o_ref,
    lists, qbuf, kbuf, kext, vext, mask, score, part_out, part_in,
    local_sem, qsend, qrecv, psend, precv, ready,
):
    me = lax.axis_index("ctx")
    grp = lax.axis_index("grp")
    me_bits, grp_bits = bits_of(me, n), bits_of(grp, ng)
    targets = [xor(grp_bits, j, ng) for j in range(ng)]
    own_rows = qbuf.shape[1]
    group_rows = QPK * own_rows
    tokens = kbuf.shape[0]
    message = part_in.shape[2]
    out_rows = own_rows // ng
    piece_rows = QPK * out_rows
    row_count = mask.shape[0]
    scale = 1.0 / math.sqrt(HD)
    log2_scale = scale * math.log2(math.e)

    barrier = pltpu.get_barrier_semaphore()
    for k in range(1, n):
        pl.semaphore_signal(barrier, inc=1, device_id={"ctx": xor(me_bits, k, n)}, device_id_type=MESH)
    for j in range(1, ng):
        pl.semaphore_signal(barrier, inc=1, device_id={"grp": targets[j]}, device_id_type=MESH)

    load_q = pltpu.make_async_copy(q_ref, qbuf.at[0], local_sem.at[0])
    load_b = pltpu.make_async_copy(b_ref, lists, local_sem.at[1])
    load_q.start()
    load_b.start()
    part_tokens = tokens // LOADS
    load_k, load_v = [], []
    for i in range(LOADS):
        at = slice(i * part_tokens, (i + 1) * part_tokens)
        load_k.append(pltpu.make_async_copy(k_ref.at[at], kbuf.at[at], local_sem.at[2 + i]))
        load_v.append(pltpu.make_async_copy(v_ref.at[at], vext.at[at, 0:HD], local_sem.at[2 + LOADS + i]))
    for copy in load_k + load_v:
        copy.start()

    def query_copy(k):
        return pltpu.make_async_remote_copy(
            src_ref=qbuf.at[0], dst_ref=qbuf.at[k], send_sem=qsend.at[k], recv_sem=qrecv.at[k],
            device_id={"ctx": xor(me_bits, k, n)}, device_id_type=MESH,
        )

    def part_copy(k, j):
        target = targets[j]
        return pltpu.make_async_remote_copy(
            src_ref=part_out.at[k, pl.ds(pl.multiple_of(target * message, PAD), message)],
            dst_ref=part_in.at[k, j], send_sem=psend.at[k, j], recv_sem=precv.at[k, j],
            device_id={"ctx": xor(me_bits, k, n), "grp": target}, device_id_type=MESH,
        )

    sub = lax.broadcasted_iota(jnp.int32, (LANES, BLOCK), 0)
    for b in range(tokens // BLOCK):
        kext[HD:, b * BLOCK:(b + 1) * BLOCK] = jnp.where(sub == b, 1.0, 0.0).astype(jnp.bfloat16)
    vext[:, HD:] = jnp.ones((tokens, LANES), jnp.bfloat16)
    diag = (
        lax.broadcasted_iota(jnp.int32, (group_rows, LANES), 0)
        == lax.broadcasted_iota(jnp.int32, (group_rows, LANES), 1)
    )
    pad_row = lax.broadcasted_iota(jnp.int32, (PAD, LANES), 0)

    to_row = lax.broadcasted_iota(jnp.int32, (ng * message, group_rows + PAD), 0)
    from_row = lax.broadcasted_iota(jnp.int32, (ng * message, group_rows + PAD), 1)
    message_bits, piece_bits = message.bit_length() - 1, out_rows.bit_length() - 1
    place = to_row & (message - 1)
    wanted = (place >> piece_bits) * own_rows + (to_row >> message_bits) * out_rows + (place & (out_rows - 1))
    wanted = jnp.where(place < piece_rows, wanted, place - piece_rows + group_rows)
    wanted = jnp.where(place < piece_rows + 3, wanted, -1)
    order = jnp.where(from_row == wanted, 1.0, 0.0).astype(jnp.bfloat16)

    pl.semaphore_wait(barrier, n - 1 + ng - 1)
    for j in range(1, ng):
        pl.semaphore_signal(ready, inc=1, device_id={"grp": targets[j]}, device_id_type=MESH)
    load_q.wait()
    for k in range(n - 1, 0, -1):
        query_copy(k).start()

    load_b.wait()
    listed = lists[...]
    block_row = lax.broadcasted_iota(jnp.int32, (tokens // BLOCK, row_count), 0)
    hit = block_row == listed[0:1, :]
    for i in range(1, listed.shape[0]):
        hit = hit | (block_row == listed[i:i + 1, :])
    bias = jnp.where(hit, 0.0, NEG)
    unused = jnp.zeros((LANES - tokens // BLOCK, row_count), jnp.float32)
    mask[...] = jnp.transpose(jnp.concatenate([bias, unused], axis=0)).astype(jnp.bfloat16)

    for i in range(LOADS):
        load_k[i].wait()
        for c in range(i * part_tokens, (i + 1) * part_tokens, BLOCK):
            at = slice(c, c + BLOCK)
            kext[0:HD, at] = jnp.transpose(kbuf[at, :].astype(jnp.float32)).astype(jnp.bfloat16)
    for copy in load_v:
        copy.wait()
    pl.semaphore_wait(ready, ng - 1)

    turns = n // SLOTS_PER_TURN

    def turn(step, carry):
        t = turns - 1 - step
        pieces = []
        for u in range(SLOTS_PER_TURN):
            k = t * SLOTS_PER_TURN + u

            if isinstance(k, int):
                if k > 0:
                    query_copy(k).wait_recv()
            else:
                pl.when(k > 0)(lambda: query_copy(k).wait_recv())

            owner = xor(me_bits, k, n)
            bias = mask[pl.ds(pl.multiple_of(owner * own_rows, own_rows), own_rows), :]
            rows = qbuf[k]
            for h in range(QPK):
                pieces.append(jnp.concatenate([rows[:, h * HD:(h + 1) * HD], bias], axis=1))
        query = jnp.concatenate(pieces, axis=0)
        top = None
        for c in range(0, tokens, CHUNK):
            s = jnp.dot(query, kext[:, c:c + CHUNK], preferred_element_type=jnp.float32)
            score[:, c:c + CHUNK] = s
            for i in range(0, CHUNK, LANES):
                part = s[:, i:i + LANES]
                top = part if top is None else jnp.maximum(top, part)
        top = jnp.max(top, axis=1, keepdims=True)
        total = None
        for c in range(0, tokens, CHUNK):
            w = jnp.exp2(((score[:, c:c + CHUNK] - top) * log2_scale).astype(jnp.bfloat16))
            piece = jnp.dot(w, vext[c:c + CHUNK, :], preferred_element_type=jnp.float32)
            total = piece if total is None else total + piece
        weight = total[:, HD:]
        part = (total[:, :HD] / weight).astype(jnp.bfloat16)
        lse = top * scale + jnp.log(weight)
        for u in range(SLOTS_PER_TURN):
            k = t * SLOTS_PER_TURN + u
            at = slice(u * group_rows, (u + 1) * group_rows)
            line = jnp.sum(jnp.where(diag, lse[at], 0.0), axis=0, keepdims=True)
            high = line.astype(jnp.bfloat16).astype(jnp.float32)
            mid = (line - high).astype(jnp.bfloat16).astype(jnp.float32)
            low = line - high - mid
            tail = jnp.where(pad_row == 0, high, jnp.where(pad_row == 1, mid, jnp.where(pad_row == 2, low, 0.0)))
            block = jnp.concatenate([part[at], tail.astype(jnp.bfloat16)], axis=0)
            part_out[k] = jnp.dot(order, block, preferred_element_type=jnp.float32).astype(jnp.bfloat16)
            for j in range(1, ng):
                part_copy(k, j).start()

            if isinstance(k, int):
                if k > 0:
                    part_copy(k, 0).start()
            else:
                pl.when(k > 0)(lambda: part_copy(k, 0).start())

        return carry

    if turns <= UNROLL:
        for step in range(turns):
            turn(step, 0)
    else:
        lax.fori_loop(0, turns, turn, 0)

    part_in[0, 0] = part_out[0, pl.ds(pl.multiple_of(grp * message, PAD), message), :]
    width = QPK * HD
    for j in range(ng):
        for k in range(n):
            if (k, j) != (0, 0):
                part_copy(k, j).wait_recv()
        lines = [
            jnp.sum(part_in[k, j, piece_rows:, :].astype(jnp.float32), axis=0, keepdims=True) for k in range(n)
        ]
        best = functools.reduce(jnp.maximum, lines)
        factors = [jnp.exp(x - best) for x in lines]
        denominator = sum(factors[1:], factors[0])
        factors.append(jnp.zeros((LANES - n, LANES), jnp.float32))
        columns = jnp.transpose(jnp.concatenate(factors, axis=0) / denominator)
        picks = []
        for h in range(QPK):
            rows = columns[h * own_rows:(h + 1) * own_rows]
            mine = rows[0:out_rows]
            for g in range(1, ng):
                mine = jnp.where(grp == g, rows[g * out_rows:(g + 1) * out_rows], mine)
            picks.append(mine)
        columns = jnp.concatenate(picks, axis=0)
        result = None
        for k in range(n):
            piece = part_in[k, j].astype(jnp.float32)[0:piece_rows] * columns[:, k:k + 1]
            result = piece if result is None else result + piece
        origin = targets[j]
        result = jnp.concatenate([result[h * out_rows:(h + 1) * out_rows] for h in range(QPK)], axis=1)
        o_ref[:, pl.ds(pl.multiple_of(origin * width, LANES), width)] = result.astype(jnp.bfloat16)

    for k in range(n):
        if k > 0:
            query_copy(k).wait_send()
        for j in range(ng):
            if (k, j) != (0, 0):
                part_copy(k, j).wait_send()


def per_device(n, ng, query, keys, values, blocks):
    own_rows, width = query.shape
    tokens = keys.shape[0]
    rows = blocks.shape[0]
    message = -(-(QPK * (own_rows // ng) + 3) // PAD) * PAD
    any_spec = pl.BlockSpec(memory_space=pl.ANY)
    vmem_spec = pl.BlockSpec(memory_space=pltpu.VMEM)
    return pl.pallas_call(
        functools.partial(kernel, n, ng),
        out_shape=jax.ShapeDtypeStruct((own_rows // ng, width * ng), jnp.bfloat16),
        in_specs=[any_spec] * 4,
        out_specs=vmem_spec,
        scratch_shapes=[
            pltpu.VMEM((blocks.shape[2], rows), jnp.int32),
            pltpu.VMEM((n, own_rows, width), jnp.bfloat16),
            pltpu.VMEM((tokens, HD), jnp.bfloat16),
            pltpu.VMEM((2 * HD, tokens), jnp.bfloat16),
            pltpu.VMEM((tokens, 2 * HD), jnp.bfloat16),
            pltpu.VMEM((rows, LANES), jnp.bfloat16),
            pltpu.VMEM((SLOTS_PER_TURN * QPK * own_rows, tokens), jnp.float32),
            pltpu.VMEM((n, ng * message, HD), jnp.bfloat16),
            pltpu.VMEM((n, ng, message, HD), jnp.bfloat16),
            pltpu.SemaphoreType.DMA((2 + 2 * LOADS,)),
            pltpu.SemaphoreType.DMA((n,)),
            pltpu.SemaphoreType.DMA((n,)),
            pltpu.SemaphoreType.DMA((n, ng)),
            pltpu.SemaphoreType.DMA((n, ng)),
            pltpu.SemaphoreType.REGULAR,
        ],
        compiler_params=pltpu.CompilerParams(
            collective_id=0, has_side_effects=True, vmem_limit_bytes=60 * 1024 * 1024
        ),
    )(query, keys, values, jnp.transpose(blocks, (1, 2, 0))[0])


def solution(mesh):
    placed = (P("ctx", "grp"), P("ctx", "grp"), P("ctx", "grp"), P(None, "ctx", None))
    body = functools.partial(per_device, mesh.shape["ctx"], mesh.shape["grp"])
    return jax.shard_map(
        body, mesh=mesh, in_specs=placed, out_specs=P(("ctx", "grp"), None), check_vma=False
    )
```

```python
import functools
import math

import jax
import jax.numpy as jnp
from jax import lax
from jax.experimental import pallas as pl
from jax.experimental.pallas import tpu as pltpu
from jax.sharding import PartitionSpec as P

HD = 128
QPK = 5
BLOCK = 128
LANES = 128
NEG = -1e30
PAD = 16
SLOTS_PER_TURN = 2
CHUNK = 1024
LOADS = 4
UNROLL = 4
MESH = pl.DeviceIdType.MESH


def bits_of(a, n):
    bits, bit = [], 1
    while bit < n:
        bits.append(lax.rem(lax.div(a, bit), 2) if not isinstance(a, int) else (a // bit) % 2)
        bit *= 2
    return bits


def xor(a_bits, b, n):
    total = 0
    for i, (x, y) in enumerate(zip(a_bits, bits_of(b, n))):
        if isinstance(y, int):
            total = total + (1 << i) * (1 - x if y else x)
        else:
            total = total + (1 << i) * (x + y - 2 * x * y)
    return total


def kernel(
    n, ng, q_ref, k_ref, v_ref, b_ref, part_in,
    lists, qbuf, kbuf, kext, vext, mask, score, part_out,
    local_sem, qsend, qrecv, psend, precv, ready,
):
    me = lax.axis_index("ctx")
    grp = lax.axis_index("grp")
    me_bits, grp_bits = bits_of(me, n), bits_of(grp, ng)
    targets = [xor(grp_bits, j, ng) for j in range(ng)]
    own_rows = qbuf.shape[1]
    group_rows = QPK * own_rows
    tokens = kbuf.shape[0]
    message = part_in.shape[2]
    out_rows = own_rows // ng
    piece_rows = QPK * out_rows
    row_count = mask.shape[0]
    scale = 1.0 / math.sqrt(HD)

    barrier = pltpu.get_barrier_semaphore()
    for k in range(1, n):
        pl.semaphore_signal(barrier, inc=1, device_id={"ctx": xor(me_bits, k, n)}, device_id_type=MESH)
    for j in range(1, ng):
        pl.semaphore_signal(barrier, inc=1, device_id={"grp": targets[j]}, device_id_type=MESH)

    load_q = pltpu.make_async_copy(q_ref, qbuf.at[0], local_sem.at[0])
    load_b = pltpu.make_async_copy(b_ref, lists, local_sem.at[1])
    load_q.start()
    load_b.start()
    part_tokens = tokens // LOADS
    load_k, load_v = [], []
    for i in range(LOADS):
        at = slice(i * part_tokens, (i + 1) * part_tokens)
        load_k.append(pltpu.make_async_copy(k_ref.at[at], kbuf.at[at], local_sem.at[2 + i]))
        load_v.append(pltpu.make_async_copy(v_ref.at[at], vext.at[at, 0:HD], local_sem.at[2 + LOADS + i]))
    for copy in load_k + load_v:
        copy.start()

    def query_copy(k):
        return pltpu.make_async_remote_copy(
            src_ref=qbuf.at[0], dst_ref=qbuf.at[k], send_sem=qsend, recv_sem=qrecv.at[k],
            device_id={"ctx": xor(me_bits, k, n)}, device_id_type=MESH,
        )

    def part_copy(k, j):
        target = targets[j]
        return pltpu.make_async_remote_copy(
            src_ref=part_out.at[k, pl.ds(pl.multiple_of(target * message, PAD), message)],
            dst_ref=part_in.at[k, j], send_sem=psend.at[0 if isinstance(k, int) and k == 0 else 1], recv_sem=precv,
            device_id={"ctx": xor(me_bits, k, n), "grp": target}, device_id_type=MESH,
        )

    def part_keep():
        return pltpu.make_async_copy(
            part_out.at[0, pl.ds(pl.multiple_of(grp * message, PAD), message)], part_in.at[0, 0], precv
        )

    sub = lax.broadcasted_iota(jnp.int32, (LANES, BLOCK), 0)
    for b in range(tokens // BLOCK):
        kext[HD:, b * BLOCK:(b + 1) * BLOCK] = jnp.where(sub == b, 1.0, 0.0).astype(jnp.bfloat16)
    vext[:, HD:] = jnp.ones((tokens, LANES), jnp.bfloat16)
    diag = (
        lax.broadcasted_iota(jnp.int32, (group_rows, LANES), 0)
        == lax.broadcasted_iota(jnp.int32, (group_rows, LANES), 1)
    )
    pad_row = lax.broadcasted_iota(jnp.int32, (PAD, LANES), 0)

    to_row = lax.broadcasted_iota(jnp.int32, (ng * message, group_rows + PAD), 0)
    from_row = lax.broadcasted_iota(jnp.int32, (ng * message, group_rows + PAD), 1)
    message_bits, piece_bits = message.bit_length() - 1, out_rows.bit_length() - 1
    place = to_row & (message - 1)
    wanted = (place >> piece_bits) * own_rows + (to_row >> message_bits) * out_rows + (place & (out_rows - 1))
    wanted = jnp.where(place < piece_rows, wanted, place - piece_rows + group_rows)
    wanted = jnp.where(place < piece_rows + 3, wanted, -1)
    order = jnp.where(from_row == wanted, 1.0, 0.0).astype(jnp.bfloat16)

    pl.semaphore_wait(barrier, n - 1 + ng - 1)
    for j in range(1, ng):
        pl.semaphore_signal(ready, inc=1, device_id={"grp": targets[j]}, device_id_type=MESH)
    load_q.wait()
    for k in range(n - 1, 0, -1):
        query_copy(k).start()

    load_b.wait()
    listed = lists[...]
    block_row = lax.broadcasted_iota(jnp.int32, (tokens // BLOCK, row_count), 0)
    hit = block_row == listed[0:1, :]
    for i in range(1, listed.shape[0]):
        hit = hit | (block_row == listed[i:i + 1, :])
    bias = jnp.where(hit, 0.0, NEG)
    unused = jnp.zeros((LANES - tokens // BLOCK, row_count), jnp.float32)
    mask[...] = jnp.transpose(jnp.concatenate([bias, unused], axis=0)).astype(jnp.bfloat16)

    for i in range(LOADS):
        load_k[i].wait()
        for c in range(i * part_tokens, (i + 1) * part_tokens, BLOCK):
            at = slice(c, c + BLOCK)
            kext[0:HD, at] = jnp.transpose(kbuf[at, :].astype(jnp.float32)).astype(jnp.bfloat16)
    for copy in load_v:
        copy.wait()
    pl.semaphore_wait(ready, ng - 1)

    turns = n // SLOTS_PER_TURN

    def turn(step, carry):
        t = turns - 1 - step
        pieces = []
        for u in range(SLOTS_PER_TURN):
            k = t * SLOTS_PER_TURN + u

            if isinstance(k, int):
                if k > 0:
                    query_copy(k).wait_recv()
            else:
                pl.when(k > 0)(lambda: query_copy(k).wait_recv())

            owner = xor(me_bits, k, n)
            bias = mask[pl.ds(pl.multiple_of(owner * own_rows, own_rows), own_rows), :]
            rows = qbuf[k]
            for h in range(QPK):
                pieces.append(jnp.concatenate([rows[:, h * HD:(h + 1) * HD], bias], axis=1))
        query = jnp.concatenate(pieces, axis=0)
        top = None
        for c in range(0, tokens, CHUNK):
            s = jnp.dot(query, kext[:, c:c + CHUNK], preferred_element_type=jnp.float32)
            score[:, c:c + CHUNK] = s
            for i in range(0, CHUNK, LANES):
                part = s[:, i:i + LANES]
                top = part if top is None else jnp.maximum(top, part)
        top = jnp.max(top, axis=1, keepdims=True)
        total = None
        for c in range(0, tokens, CHUNK):
            w = jnp.exp((score[:, c:c + CHUNK] - top) * scale).astype(jnp.bfloat16)
            piece = jnp.dot(w, vext[c:c + CHUNK, :], preferred_element_type=jnp.float32)
            total = piece if total is None else total + piece
        weight = total[:, HD:]
        part = (total[:, :HD] / weight).astype(jnp.bfloat16)
        lse = top * scale + jnp.log(weight)
        for u in range(SLOTS_PER_TURN):
            k = t * SLOTS_PER_TURN + u
            at = slice(u * group_rows, (u + 1) * group_rows)
            line = jnp.sum(jnp.where(diag, lse[at], 0.0), axis=0, keepdims=True)
            high = line.astype(jnp.bfloat16).astype(jnp.float32)
            mid = (line - high).astype(jnp.bfloat16).astype(jnp.float32)
            low = line - high - mid
            tail = jnp.where(pad_row == 0, high, jnp.where(pad_row == 1, mid, jnp.where(pad_row == 2, low, 0.0)))
            block = jnp.concatenate([part[at], tail.astype(jnp.bfloat16)], axis=0)
            part_out[k] = jnp.dot(order, block, preferred_element_type=jnp.float32).astype(jnp.bfloat16)
            for j in range(1, ng):
                part_copy(k, j).start()
            if isinstance(k, int) and k == 0:
                part_keep().start()
            else:
                part_copy(k, 0).start()

        return carry

    if turns <= UNROLL:
        for step in range(turns):
            turn(step, 0)
    else:
        lax.fori_loop(0, turns - 1, turn, 0)
        turn(turns - 1, 0)

    for finished, semaphore in (
        (part_in, precv), (part_out.at[0, pl.ds(0, (ng - 1) * message)], psend.at[0]),
        (part_out.at[pl.ds(1, n - 1)], psend.at[1]), (qbuf.at[pl.ds(1, n - 1)], qsend),
    ):
        pltpu.make_async_copy(finished, finished, semaphore).wait()


def combine(n, ng, own_rows, part_in, o_ref):
    grp = lax.axis_index("grp")
    grp_bits = bits_of(grp, ng)
    out_rows = own_rows // ng
    piece_rows = QPK * out_rows
    width = QPK * HD
    for j in range(ng):
        lines = [
            jnp.sum(part_in[k, j, piece_rows:, :].astype(jnp.float32), axis=0, keepdims=True) for k in range(n)
        ]
        best = functools.reduce(jnp.maximum, lines)
        factors = [jnp.exp(x - best) for x in lines]
        denominator = sum(factors[1:], factors[0])
        factors.append(jnp.zeros((LANES - n, LANES), jnp.float32))
        columns = jnp.transpose(jnp.concatenate(factors, axis=0) / denominator)
        picks = []
        for h in range(QPK):
            rows = columns[h * own_rows:(h + 1) * own_rows]
            mine = rows[0:out_rows]
            for g in range(1, ng):
                mine = jnp.where(grp == g, rows[g * out_rows:(g + 1) * out_rows], mine)
            picks.append(mine)
        columns = jnp.concatenate(picks, axis=0)
        result = None
        for k in range(n):
            piece = part_in[k, j].astype(jnp.float32)[0:piece_rows] * columns[:, k:k + 1]
            result = piece if result is None else result + piece
        origin = xor(grp_bits, j, ng)
        result = jnp.concatenate([result[h * out_rows:(h + 1) * out_rows] for h in range(QPK)], axis=1)
        o_ref[:, pl.ds(pl.multiple_of(origin * width, LANES), width)] = result.astype(jnp.bfloat16)


def per_device(n, ng, query, keys, values, blocks):
    own_rows, width = query.shape
    tokens = keys.shape[0]
    rows = blocks.shape[0]
    message = -(-(QPK * (own_rows // ng) + 3) // PAD) * PAD
    any_spec = pl.BlockSpec(memory_space=pl.ANY)
    vmem_spec = pl.BlockSpec(memory_space=pltpu.VMEM)
    parts = pl.pallas_call(
        functools.partial(kernel, n, ng),
        out_shape=jax.ShapeDtypeStruct((n, ng, message, HD), jnp.bfloat16),
        in_specs=[any_spec] * 4,
        out_specs=any_spec,
        scratch_shapes=[
            pltpu.VMEM((blocks.shape[2], rows), jnp.int32),
            pltpu.VMEM((n, own_rows, width), jnp.bfloat16),
            pltpu.VMEM((tokens, HD), jnp.bfloat16),
            pltpu.VMEM((2 * HD, tokens), jnp.bfloat16),
            pltpu.VMEM((tokens, 2 * HD), jnp.bfloat16),
            pltpu.VMEM((rows, LANES), jnp.bfloat16),
            pltpu.VMEM((SLOTS_PER_TURN * QPK * own_rows, tokens), jnp.float32),
            pltpu.VMEM((n, ng * message, HD), jnp.bfloat16),
            pltpu.SemaphoreType.DMA((2 + 2 * LOADS,)),
            pltpu.SemaphoreType.DMA,
            pltpu.SemaphoreType.DMA((n,)),
            pltpu.SemaphoreType.DMA((2,)),
            pltpu.SemaphoreType.DMA,
            pltpu.SemaphoreType.REGULAR,
        ],
        compiler_params=pltpu.CompilerParams(
            collective_id=0, has_side_effects=True, vmem_limit_bytes=60 * 1024 * 1024
        ),
    )(query, keys, values, jnp.transpose(blocks, (1, 2, 0))[0])
    return pl.pallas_call(
        functools.partial(combine, n, ng, own_rows),
        out_shape=jax.ShapeDtypeStruct((own_rows // ng, width * ng), jnp.bfloat16),
        in_specs=[vmem_spec],
        out_specs=vmem_spec,
    )(parts)


def solution(mesh):
    placed = (P("ctx", "grp"), P("ctx", "grp"), P("ctx", "grp"), P(None, "ctx", None))
    body = functools.partial(per_device, mesh.shape["ctx"], mesh.shape["grp"])
    return jax.shard_map(
        body, mesh=mesh, in_specs=placed, out_specs=P(("ctx", "grp"), None), check_vma=False
    )
```

```python
import functools
import math

import jax
import jax.numpy as jnp
from jax import lax
from jax.experimental import pallas as pl
from jax.experimental.pallas import tpu as pltpu
from jax.sharding import PartitionSpec as P

HD = 128
QPK = 5
BLOCK = 128
LANES = 128
NEG = -1e30
PAD = 16
SLOTS_PER_TURN = 2
CHUNK = 1024
LOADS = 4
UNROLL = 4
MESH = pl.DeviceIdType.MESH


def bits_of(a, n):
    bits, bit = [], 1
    while bit < n:
        bits.append(lax.rem(lax.div(a, bit), 2) if not isinstance(a, int) else (a // bit) % 2)
        bit *= 2
    return bits


def xor(a_bits, b, n):
    total = 0
    for i, (x, y) in enumerate(zip(a_bits, bits_of(b, n))):
        if isinstance(y, int):
            total = total + (1 << i) * (1 - x if y else x)
        else:
            total = total + (1 << i) * (x + y - 2 * x * y)
    return total


def kernel(
    n, ng, q_ref, k_ref, v_ref, b_ref, part_in,
    lists, qbuf, kbuf, kext, vext, mask, score, part_out,
    local_sem, qsend, qrecv, psend, precv, ready,
):
    me = lax.axis_index("ctx")
    grp = lax.axis_index("grp")
    me_bits, grp_bits = bits_of(me, n), bits_of(grp, ng)
    targets = [xor(grp_bits, j, ng) for j in range(ng)]
    own_rows = qbuf.shape[1]
    group_rows = QPK * own_rows
    tokens = kbuf.shape[0]
    message = part_in.shape[2]
    out_rows = own_rows // ng
    piece_rows = QPK * out_rows
    row_count = mask.shape[0]
    scale = 1.0 / math.sqrt(HD)

    barrier = pltpu.get_barrier_semaphore()
    for k in range(1, n):
        pl.semaphore_signal(barrier, inc=1, device_id={"ctx": xor(me_bits, k, n)}, device_id_type=MESH)
    for j in range(1, ng):
        pl.semaphore_signal(barrier, inc=1, device_id={"grp": targets[j]}, device_id_type=MESH)

    load_q = pltpu.make_async_copy(q_ref, qbuf.at[0], local_sem.at[0])
    load_b = pltpu.make_async_copy(b_ref, lists, local_sem.at[1])
    load_q.start()
    load_b.start()
    part_tokens = tokens // LOADS
    load_k, load_v = [], []
    for i in range(LOADS):
        at = slice(i * part_tokens, (i + 1) * part_tokens)
        load_k.append(pltpu.make_async_copy(k_ref.at[at], kbuf.at[at], local_sem.at[2 + i]))
        load_v.append(pltpu.make_async_copy(v_ref.at[at], vext.at[at, 0:HD], local_sem.at[2 + LOADS + i]))
    for copy in load_k + load_v:
        copy.start()

    def query_copy(k):
        return pltpu.make_async_remote_copy(
            src_ref=qbuf.at[0], dst_ref=qbuf.at[k], send_sem=qsend, recv_sem=qrecv.at[k],
            device_id={"ctx": xor(me_bits, k, n)}, device_id_type=MESH,
        )

    def part_copy(k, j):
        target = targets[j]
        return pltpu.make_async_remote_copy(
            src_ref=part_out.at[k, pl.ds(pl.multiple_of(target * message, PAD), message)],
            dst_ref=part_in.at[k, j], send_sem=psend.at[0 if isinstance(k, int) and k == 0 else 1], recv_sem=precv,
            device_id={"ctx": xor(me_bits, k, n), "grp": target}, device_id_type=MESH,
        )

    def part_keep():
        return pltpu.make_async_copy(
            part_out.at[0, pl.ds(pl.multiple_of(grp * message, PAD), message)], part_in.at[0, 0], precv
        )

    sub = lax.broadcasted_iota(jnp.int32, (LANES, BLOCK), 0)
    for b in range(tokens // BLOCK):
        kext[HD:, b * BLOCK:(b + 1) * BLOCK] = jnp.where(sub == b, 1.0, 0.0).astype(jnp.bfloat16)
    vext[:, HD:] = jnp.ones((tokens, LANES), jnp.bfloat16)
    diag = (
        lax.broadcasted_iota(jnp.int32, (group_rows, LANES), 0)
        == lax.broadcasted_iota(jnp.int32, (group_rows, LANES), 1)
    )
    pad_row = lax.broadcasted_iota(jnp.int32, (PAD, LANES), 0)

    to_row = lax.broadcasted_iota(jnp.int32, (ng * message, group_rows + PAD), 0)
    from_row = lax.broadcasted_iota(jnp.int32, (ng * message, group_rows + PAD), 1)
    message_bits, piece_bits = message.bit_length() - 1, out_rows.bit_length() - 1
    place = to_row & (message - 1)
    wanted = (place >> piece_bits) * own_rows + (to_row >> message_bits) * out_rows + (place & (out_rows - 1))
    wanted = jnp.where(place < piece_rows, wanted, place - piece_rows + group_rows)
    wanted = jnp.where(place < piece_rows + 3, wanted, -1)
    order = jnp.where(from_row == wanted, 1.0, 0.0).astype(jnp.bfloat16)

    pl.semaphore_wait(barrier, n - 1 + ng - 1)
    for j in range(1, ng):
        pl.semaphore_signal(ready, inc=1, device_id={"grp": targets[j]}, device_id_type=MESH)
    load_q.wait()
    for k in range(n - 1, 0, -1):
        query_copy(k).start()

    load_b.wait()
    listed = lists[...]
    block_row = lax.broadcasted_iota(jnp.int32, (tokens // BLOCK, row_count), 0)
    hit = block_row == listed[0:1, :]
    for i in range(1, listed.shape[0]):
        hit = hit | (block_row == listed[i:i + 1, :])
    bias = jnp.where(hit, 0.0, NEG)
    unused = jnp.zeros((LANES - tokens // BLOCK, row_count), jnp.float32)
    mask[...] = jnp.transpose(jnp.concatenate([bias, unused], axis=0)).astype(jnp.bfloat16)

    for i in range(LOADS):
        load_k[i].wait()
        for c in range(i * part_tokens, (i + 1) * part_tokens, BLOCK):
            at = slice(c, c + BLOCK)
            kext[0:HD, at] = jnp.transpose(kbuf[at, :].astype(jnp.float32)).astype(jnp.bfloat16)
    for copy in load_v:
        copy.wait()
    pl.semaphore_wait(ready, ng - 1)

    turns = n // SLOTS_PER_TURN

    def prepare(t):
        pieces = []
        for u in range(SLOTS_PER_TURN):
            k = t * SLOTS_PER_TURN + u

            if isinstance(k, int):
                if k > 0:
                    query_copy(k).wait_recv()
            else:
                pl.when(k > 0)(lambda: query_copy(k).wait_recv())

            owner = xor(me_bits, k, n)
            bias = mask[pl.ds(pl.multiple_of(owner * own_rows, own_rows), own_rows), :]
            rows = qbuf[k]
            for h in range(QPK):
                pieces.append(jnp.concatenate([rows[:, h * HD:(h + 1) * HD], bias], axis=1))
        query = jnp.concatenate(pieces, axis=0)
        return query

    def scores(query, buffer, c, top):
        s = jnp.dot(query, kext[:, c:c + CHUNK], preferred_element_type=jnp.float32)
        score[buffer, :, c:c + CHUNK] = s
        for i in range(0, CHUNK, LANES):
            part = s[:, i:i + LANES]
            top = part if top is None else jnp.maximum(top, part)
        return top

    def attend(buffer, c, top, total):
        w = jnp.exp((score[buffer, :, c:c + CHUNK] - top) * scale).astype(jnp.bfloat16)
        piece = jnp.dot(w, vext[c:c + CHUNK, :], preferred_element_type=jnp.float32)
        return piece if total is None else total + piece

    def finish(t, top, total):
        weight = total[:, HD:]
        part = (total[:, :HD] / weight).astype(jnp.bfloat16)
        lse = top * scale + jnp.log(weight)
        for u in range(SLOTS_PER_TURN):
            k = t * SLOTS_PER_TURN + u
            at = slice(u * group_rows, (u + 1) * group_rows)
            line = jnp.sum(jnp.where(diag, lse[at], 0.0), axis=0, keepdims=True)
            high = line.astype(jnp.bfloat16).astype(jnp.float32)
            mid = (line - high).astype(jnp.bfloat16).astype(jnp.float32)
            low = line - high - mid
            tail = jnp.where(pad_row == 0, high, jnp.where(pad_row == 1, mid, jnp.where(pad_row == 2, low, 0.0)))
            block = jnp.concatenate([part[at], tail.astype(jnp.bfloat16)], axis=0)
            part_out[k] = jnp.dot(order, block, preferred_element_type=jnp.float32).astype(jnp.bfloat16)
            for j in range(1, ng):
                part_copy(k, j).start()
            if isinstance(k, int) and k == 0:
                part_keep().start()
            else:
                part_copy(k, 0).start()

    def turn(step, carry):
        t = turns - 1 - step
        query = prepare(t)
        top, total = None, None
        for c in range(0, tokens, CHUNK):
            top = scores(query, 0, c, top)
        top = jnp.max(top, axis=1, keepdims=True)
        for c in range(0, tokens, CHUNK):
            total = attend(0, c, top, total)
        finish(t, top, total)
        return carry

    if turns <= UNROLL:
        query, top = prepare(turns - 1), None
        for c in range(0, tokens, CHUNK):
            top = scores(query, 0, c, top)
        for step in range(turns):
            t = turns - 1 - step
            now, total, later = jnp.max(top, axis=1, keepdims=True), None, None
            if t > 0:
                query = prepare(t - 1)
            for c in range(0, tokens, CHUNK):
                if t > 0:
                    later = scores(query, (step + 1) % 2, c, later)
                total = attend(step % 2, c, now, total)
            finish(t, now, total)
            top = later
    else:
        lax.fori_loop(0, turns - 1, turn, 0)
        turn(turns - 1, 0)

    for finished, semaphore in (
        (part_in, precv), (part_out.at[0, pl.ds(0, (ng - 1) * message)], psend.at[0]),
        (part_out.at[pl.ds(1, n - 1)], psend.at[1]), (qbuf.at[pl.ds(1, n - 1)], qsend),
    ):
        pltpu.make_async_copy(finished, finished, semaphore).wait()


def combine(n, ng, own_rows, part_in, o_ref):
    grp = lax.axis_index("grp")
    grp_bits = bits_of(grp, ng)
    out_rows = own_rows // ng
    piece_rows = QPK * out_rows
    width = QPK * HD
    for j in range(ng):
        lines = [
            jnp.sum(part_in[k, j, piece_rows:, :].astype(jnp.float32), axis=0, keepdims=True) for k in range(n)
        ]
        best = functools.reduce(jnp.maximum, lines)
        factors = [jnp.exp(x - best) for x in lines]
        denominator = sum(factors[1:], factors[0])
        factors.append(jnp.zeros((LANES - n, LANES), jnp.float32))
        columns = jnp.transpose(jnp.concatenate(factors, axis=0) / denominator)
        picks = []
        for h in range(QPK):
            rows = columns[h * own_rows:(h + 1) * own_rows]
            mine = rows[0:out_rows]
            for g in range(1, ng):
                mine = jnp.where(grp == g, rows[g * out_rows:(g + 1) * out_rows], mine)
            picks.append(mine)
        columns = jnp.concatenate(picks, axis=0)
        result = None
        for k in range(n):
            piece = part_in[k, j].astype(jnp.float32)[0:piece_rows] * columns[:, k:k + 1]
            result = piece if result is None else result + piece
        origin = xor(grp_bits, j, ng)
        result = jnp.concatenate([result[h * out_rows:(h + 1) * out_rows] for h in range(QPK)], axis=1)
        o_ref[:, pl.ds(pl.multiple_of(origin * width, LANES), width)] = result.astype(jnp.bfloat16)


def per_device(n, ng, query, keys, values, blocks):
    own_rows, width = query.shape
    tokens = keys.shape[0]
    rows = blocks.shape[0]
    message = -(-(QPK * (own_rows // ng) + 3) // PAD) * PAD
    any_spec = pl.BlockSpec(memory_space=pl.ANY)
    vmem_spec = pl.BlockSpec(memory_space=pltpu.VMEM)
    parts = pl.pallas_call(
        functools.partial(kernel, n, ng),
        out_shape=jax.ShapeDtypeStruct((n, ng, message, HD), jnp.bfloat16),
        in_specs=[any_spec] * 4,
        out_specs=any_spec,
        scratch_shapes=[
            pltpu.VMEM((blocks.shape[2], rows), jnp.int32),
            pltpu.VMEM((n, own_rows, width), jnp.bfloat16),
            pltpu.VMEM((tokens, HD), jnp.bfloat16),
            pltpu.VMEM((2 * HD, tokens), jnp.bfloat16),
            pltpu.VMEM((tokens, 2 * HD), jnp.bfloat16),
            pltpu.VMEM((rows, LANES), jnp.bfloat16),
            pltpu.VMEM((2, SLOTS_PER_TURN * QPK * own_rows, tokens), jnp.float32),
            pltpu.VMEM((n, ng * message, HD), jnp.bfloat16),
            pltpu.SemaphoreType.DMA((2 + 2 * LOADS,)),
            pltpu.SemaphoreType.DMA,
            pltpu.SemaphoreType.DMA((n,)),
            pltpu.SemaphoreType.DMA((2,)),
            pltpu.SemaphoreType.DMA,
            pltpu.SemaphoreType.REGULAR,
        ],
        compiler_params=pltpu.CompilerParams(
            collective_id=0, has_side_effects=True, vmem_limit_bytes=60 * 1024 * 1024
        ),
    )(query, keys, values, jnp.transpose(blocks, (1, 2, 0))[0])
    return pl.pallas_call(
        functools.partial(combine, n, ng, own_rows),
        out_shape=jax.ShapeDtypeStruct((own_rows // ng, width * ng), jnp.bfloat16),
        in_specs=[vmem_spec],
        out_specs=vmem_spec,
    )(parts)


def solution(mesh):
    placed = (P("ctx", "grp"), P("ctx", "grp"), P("ctx", "grp"), P(None, "ctx", None))
    body = functools.partial(per_device, mesh.shape["ctx"], mesh.shape["grp"])
    return jax.shard_map(
        body, mesh=mesh, in_specs=placed, out_specs=P(("ctx", "grp"), None), check_vma=False
    )
```
